32 devices in a mesh: parts: 2 (over y), dp: 2 (over core), tensor: 8 (over z, x).
Axes of the slice: x: 2, y: 2, z: 4, core: 2. Of those that a mesh axis runs over, the one named last changes fastest.
Arguments:
- tokens: bfloat16 [4096, 6144], P(('parts', 'dp'), 'tensor'), parts along dimension 0, may hold values from -6 to 6
- expert_index: int32 [4096, 2], P(('parts', 'dp')), parts along dimension 0, may hold values from 0 to 7, as said below
- combine_weight: float32 [4096, 2], P(('parts', 'dp')), parts along dimension 0, may hold values from 0.2 to 1
- gate_weight: bfloat16 [6144, 16384], P(None, 'tensor'), may hold values from -0.078125 to 0.078125
- up_weight: bfloat16 [6144, 16384], P(None, 'tensor'), may hold values from -0.078125 to 0.078125
- down_weight: bfloat16 [16384, 6144], P('tensor'), may hold values from -0.0625 to 0.0625
Outputs:
- mixed: bfloat16 [4096, 6144], P(('parts', 'dp'), 'tensor'), parts along dimension 0
The draws below stay inside these ranges and needn't reach their ends.
There are 2 independent parts, one for each index of `parts`. The reference program is written for one: setup_inputs(seed, part) draws one part's arguments, and reference() takes and returns one part's arrays. A program takes and returns all parts, laid end to end along the dimension named above; an argument that names none is the same for every part. Nothing has to cross between parts.
Inputs may be any that keep to these rules, and one draw needn't show every extreme that they name: `expert_index`: each row names 2 different experts. Among the tokens of one dp index (each aligned block of 1024 rows) at most 512 name expert 0, a quarter of 512 at least, and in every draw some block has exactly 512.
All inputs are finite; a program needn't handle non-finite values.
Results may differ from the reference program's by a relative error of at most 0.005.
Values may be sent and summed in bfloat16 or wider, within the bound.
No kernel may reach another device: no remote copies, remote signals or barrier semaphores. Data moves between devices by JAX's collectives and lax.ppermute only.
A program may use at most 192 MiB of HBM per device.

```python
import jax
import jax.numpy as jnp
from jax import lax

D = 6144
FF = 16384
EXPERTS = 8
TOP = 2
TOK_DEV = 1024
TOKENS = 2048
MOST = 512


def draw_expert_index(key, part):
    key = jax.random.fold_in(key, 7)
    keys = jax.random.split(key, 6)
    blocks = TOKENS // TOK_DEV
    counts = jax.random.randint(keys[0], (blocks,), max(MOST // 4, 1), MOST + 1)
    forced = jax.random.randint(keys[1], (), 0, blocks)
    counts = jnp.where(jnp.arange(blocks) == forced, MOST, counts)
    scores = jax.random.randint(keys[2], (blocks, TOK_DEV), 0, 1 << 18) * TOK_DEV + jnp.arange(TOK_DEV)[None, :]
    ordering = jnp.argsort(scores, axis=1, stable=True)
    ranking = jnp.argsort(ordering, axis=1, stable=True)
    chosen = ranking < counts[:, None]
    first_other = jax.random.randint(keys[3], (blocks, TOK_DEV), 1, EXPERTS)
    second = jax.random.randint(keys[4], (blocks, TOK_DEV), 1, EXPERTS - 1)
    second = second + (second >= first_other).astype(jnp.int32)
    leading = jnp.where(chosen, 0, second)
    flipped = jax.random.randint(keys[5], (blocks, TOK_DEV), 0, 2) == 1
    slot_a = jnp.where(flipped, first_other, leading)
    slot_b = jnp.where(flipped, leading, first_other)
    return jnp.stack([slot_a, slot_b], axis=-1).reshape(TOKENS, TOP).astype(jnp.int32)


def strengthened(drawn, stream_key, source, target, shards_of, factor):
    owner, partner = [(jnp.arange(drawn.shape[axis_at]) // (drawn.shape[axis_at] // shards_of)).reshape([-1 if axis == axis_at else 1 for axis in range(drawn.ndim)]) for axis_at in (source, target)]
    chosen = jax.random.permutation(stream_key, shards_of)[partner]
    strong = (owner == chosen) | (owner == (partner + shards_of // 2) % shards_of)
    return jnp.where(strong, factor * drawn, drawn)


def level_of(stream_key, shape, cuts, least, top_value):
    loudness, own = 1.0, jax.random.fold_in(stream_key, 6)
    for axis_at, parts in cuts:
        heights = jnp.exp(jax.random.uniform(jax.random.fold_in(own, axis_at), (parts,), jnp.float32, least / len(cuts), top_value / len(cuts)))
        loudness = loudness * jnp.repeat(heights, shape[axis_at] // parts).reshape([-1 if axis == axis_at else 1 for axis in range(len(shape))])
    return loudness


def bell_draw(rng, shape, width, bound, shards=(), kind=jnp.bfloat16):
    values = width * jax.random.normal(rng, shape, jnp.float32)
    if shards:
        values = values * level_of(rng, shape, shards, -0.22, 0.18)
    return jnp.clip(values, -bound, bound).astype(kind)


def heavy_noise(stream_key, extent, deviation, bound, cuts, heavy, held_as=jnp.bfloat16):
    entries = deviation * jax.random.normal(stream_key, extent, jnp.float32)
    if cuts:
        entries = entries * level_of(stream_key, extent, cuts, -0.22, 0.18)
    return jnp.clip(strengthened(entries, jax.random.fold_in(stream_key, 3), *heavy), -bound, bound).astype(held_as)


def setup_inputs(seed: int = 0, part: int = 0) -> dict:
    splits = jax.random.split(jax.random.key(seed), 7)
    part_keys = jax.random.split(jax.random.fold_in(splits[6], part), 7)
    tokens = bell_draw(part_keys[0], (TOKENS, D), 1.0, 6.0, ((0, 2), (1, 8)))
    expert_index = draw_expert_index(jax.random.fold_in(jax.random.fold_in(splits[6], part), 71), part)
    combine_weight = jnp.clip(0.2 + 0.8 * jax.random.uniform(part_keys[2], (TOKENS, TOP), jnp.float32) ** level_of(part_keys[2], (TOKENS, TOP), ((0, 2),), -0.2, 0.2), 0.2, 1.0)
    gate_weight = bell_draw(splits[3], (D, FF), D ** -0.5, 0.078125, ((1, 8),))
    up_weight = bell_draw(splits[4], (D, FF), D ** -0.5, 0.078125, ((1, 8),))
    down_weight = heavy_noise(splits[5], (FF, D), FF ** -0.5, 0.0625, ((0, 8),), (0, 1, 8, 2.0))
    return {"tokens": tokens, "expert_index": expert_index, "combine_weight": combine_weight, "gate_weight": gate_weight, "up_weight": up_weight, "down_weight": down_weight}


def dispatch_table(index_block, weight_block):
    chosen = index_block == 0
    routed = jnp.any(chosen, axis=1)
    factor = jnp.sum(jnp.where(chosen, weight_block, 0.0), axis=1)
    position = jnp.cumsum(routed.astype(jnp.int32)) - 1
    slot_ids = jnp.arange(MOST, dtype=jnp.int32)
    select = (position[None, :] == slot_ids[:, None]) & routed[None, :]
    token_ids = jnp.arange(index_block.shape[0], dtype=jnp.int32)
    slot_token = jnp.sum(jnp.where(select, token_ids[None, :], 0), axis=1).astype(jnp.int32)
    slot_scale = jnp.sum(jnp.where(select, factor[None, :], 0.0), axis=1)
    return slot_token, slot_scale


def reference(tokens, expert_index, combine_weight, gate_weight, up_weight, down_weight):
    blocks = TOKENS // TOK_DEV

    def one_block(inputs):
        token_block, index_block, weight_block = inputs
        slot_token, slot_scale = dispatch_table(index_block, weight_block)
        gathered = jnp.take(token_block, slot_token, axis=0)
        gate = jnp.dot(gathered, gate_weight, preferred_element_type=jnp.float32)
        up_part = jnp.dot(gathered, up_weight, preferred_element_type=jnp.float32)
        hidden = (jax.nn.silu(gate) * up_part).astype(jnp.bfloat16)
        partial_value = jnp.dot(hidden, down_weight, preferred_element_type=jnp.float32) * slot_scale[:, None]
        output = jnp.zeros((TOK_DEV, D), partial_value.dtype).at[slot_token].add(partial_value)
        return output.astype(jnp.bfloat16)

    result = lax.map(one_block, (tokens.reshape(blocks, TOK_DEV, D),
                                 expert_index.reshape(blocks, TOK_DEV, TOP),
                                 combine_weight.reshape(blocks, TOK_DEV, TOP)))
    return result.reshape(TOKENS, D)
```

```python
import functools

import jax
import jax.numpy as jnp
from jax import lax
from jax.experimental import pallas as pl
from jax.experimental.pallas import tpu as pltpu
from jax.sharding import PartitionSpec as P

MOST = 512
LANES = 128
TILE = 256
F32 = jnp.float32
BF16 = jnp.bfloat16
VMEM_BYTES = 48 * 1024 * 1024


def params():
    return pltpu.CompilerParams(vmem_limit_bytes=VMEM_BYTES)


def dot(a, b):
    return jnp.dot(a, b, preferred_element_type=F32)


def compact_kernel(routed_ref, tokens_ref, chosen_ref, slot_ref, select_ref):
    slots = select_ref.shape[0]
    groups = routed_ref.shape[0]
    routed = routed_ref[...]
    above = lax.broadcasted_iota(jnp.int32, (LANES, LANES), 0) <= lax.broadcasted_iota(
        jnp.int32, (LANES, LANES), 1
    )
    within = dot(routed.astype(BF16), jnp.where(above, 1.0, 0.0).astype(BF16))
    before = jnp.zeros((1, 1), F32)
    slot_ids = lax.broadcasted_iota(jnp.int32, (slots, LANES), 0)
    for g in range(groups):
        row = within[g : g + 1, :] + before
        before = row[:, LANES - 1 :]
        slot = jnp.where(routed[g : g + 1, :] > 0, row.astype(jnp.int32) - 1, -1)
        slot_ref[g : g + 1, :] = slot
        select_ref[:, g * LANES : (g + 1) * LANES] = jnp.where(slot_ids == slot, 1.0, 0.0).astype(BF16)
    chosen_ref[...] = dot(select_ref[...], tokens_ref[...]).astype(BF16)


def compact(routed, tokens, slots):
    count, width = tokens.shape
    groups = count // LANES
    return pl.pallas_call(
        compact_kernel,
        out_shape=(
            jax.ShapeDtypeStruct((slots, width), BF16),
            jax.ShapeDtypeStruct((groups, LANES), jnp.int32),
        ),
        scratch_shapes=[pltpu.VMEM((slots, count), BF16)],
        compiler_params=params(),
        name="compact",
    )(routed.astype(F32).reshape(groups, LANES), tokens)


def gate_up_kernel(ids_ref, *refs, pieces, first, last):
    xs, refs = refs[:pieces], refs[pieces:]
    weights = 1 if last else pieces
    gates, refs = refs[:weights], refs[weights:]
    ups, refs = refs[:weights], refs[weights:]
    if last:
        gate_in, up_in, hidden_ref = refs
        rows = xs[0].shape[0]
        for half in range(2):
            at = slice(half * rows, (half + 1) * rows)
            gate = gate_in[at, :] + dot(xs[half][...], gates[0][...])
            up = up_in[at, :] + dot(xs[half][...], ups[0][...])
            hidden_ref[at, :] = (gate / (1.0 + jnp.exp(-gate)) * up).astype(BF16)
        return
    gate = dot(xs[0][...], gates[0][...])
    up = dot(xs[0][...], ups[0][...])
    for i in range(1, pieces):
        gate += dot(xs[i][...], gates[i][...])
        up += dot(xs[i][...], ups[i][...])
    if first:
        gate_out, up_out = refs
        gate_out[...] = gate
        up_out[...] = up
    else:
        gate_in, up_in, gate_out, up_out = refs
        gate_out[...] = gate_in[...] + gate
        up_out[...] = up_in[...] + up


def gate_up(ids, steps, xs, gate_weight, up_weight, sums, last=False):
    width = xs[0].shape[1]
    hidden = gate_weight.shape[1]
    slots = xs[0].shape[0] * (2 if last else 1)
    first = sums is None
    weights = [
        pl.BlockSpec((width, TILE), functools.partial(lambda n, ids, j: (ids[j], n), j=j))
        for j in steps
    ]
    block = pl.BlockSpec((slots, TILE), lambda n, ids: (0, n))
    xspecs = [pl.BlockSpec(x.shape, lambda n, ids: (0, 0)) for x in xs]
    total = jax.ShapeDtypeStruct((slots, hidden), F32)
    in_specs = xspecs + weights + weights + ([] if first else [block, block])
    operands = [*xs, *[gate_weight] * len(steps), *[up_weight] * len(steps), *([] if first else sums)]
    aliases = {}
    if last:
        out_shape, out_specs = jax.ShapeDtypeStruct((slots, hidden), BF16), block
    else:
        out_shape, out_specs = (total, total), (block, block)
        if not first:
            at = 1 + len(operands) - 2
            aliases = {at: 0, at + 1: 1}
    flops = 4 * slots * width * hidden * len(steps)
    moved = 4 * width * hidden * len(steps) + 16 * slots * hidden
    return pl.pallas_call(
        functools.partial(gate_up_kernel, pieces=len(xs), first=first, last=last),
        grid_spec=pltpu.PrefetchScalarGridSpec(
            num_scalar_prefetch=1, grid=(hidden // TILE,), in_specs=in_specs, out_specs=out_specs
        ),
        out_shape=out_shape,
        input_output_aliases=aliases,
        compiler_params=params(),
        cost_estimate=pl.CostEstimate(flops=flops, bytes_accessed=moved, transcendentals=0),
        name="gate_up",
    )(ids, *operands)


def down_kernel(ids_ref, hidden_ref, *refs, pieces, split):
    weights, outs = refs[:pieces], refs[pieces:]
    hidden = hidden_ref[...]
    for i in range(pieces):
        value = dot(hidden, weights[i][...])
        if split:
            rows = outs[0].shape[0]
            outs[0][...] = value[:rows].astype(BF16)
            outs[1][...] = value[rows:].astype(BF16)
        else:
            outs[i][...] = value


def down(ids, steps, hidden, down_weight, width, split=False):
    slots, depth = hidden.shape
    tiles = width // TILE
    weights = [
        pl.BlockSpec((depth, TILE), functools.partial(lambda n, ids, j: (0, ids[j] * tiles + n), j=j))
        for j in steps
    ]
    if split:
        shape, kind, outs = (slots // 2, width), BF16, 2
    else:
        shape, kind, outs = (slots, width), F32, len(steps)
    return pl.pallas_call(
        functools.partial(down_kernel, pieces=len(steps), split=split),
        grid_spec=pltpu.PrefetchScalarGridSpec(
            num_scalar_prefetch=1,
            grid=(tiles,),
            in_specs=[pl.BlockSpec(hidden.shape, lambda n, ids: (0, 0))] + weights,
            out_specs=(pl.BlockSpec((shape[0], TILE), lambda n, ids: (0, n)),) * outs,
        ),
        out_shape=(jax.ShapeDtypeStruct(shape, kind),) * outs,
        compiler_params=params(),
        cost_estimate=pl.CostEstimate(
            flops=2 * slots * depth * width * len(steps),
            bytes_accessed=2 * depth * width * len(steps) + 4 * slots * width * len(steps),
            transcendentals=0,
        ),
        name="down",
    )(ids, hidden, *[down_weight] * len(steps))


def spread_kernel(place_ref, scale_ref, own_ref, right_ref, left_ref, out_ref):
    total = own_ref[...] + right_ref[...].astype(F32) + left_ref[...].astype(F32)
    scaled = (total * scale_ref[...]).astype(BF16)
    out_ref[...] = dot(place_ref[...], scaled).astype(BF16)


def spread(place, scale, own, right, left):
    count, slots = place.shape
    width = own.shape[1]
    block = pl.BlockSpec((slots, TILE), lambda n: (0, n))
    return pl.pallas_call(
        spread_kernel,
        grid=(width // TILE,),
        in_specs=[
            pl.BlockSpec(place.shape, lambda n: (0, 0)),
            pl.BlockSpec(scale.shape, lambda n: (0, 0)),
            block,
            block,
            block,
        ],
        out_specs=pl.BlockSpec((count, TILE), lambda n: (0, n)),
        out_shape=jax.ShapeDtypeStruct((count, width), BF16),
        compiler_params=params(),
        name="spread",
    )(place, scale, own, right, left)


def ring_of(size):
    return [*range(0, size, 2), *range(size - 1, 0, -2)]


def ring_plan(size, slots, tokens, routed, factor, gate_weight, up_weight, down_weight):
    width = tokens.shape[1]
    half = size // 2
    order = ring_of(size)
    table = [[order[(order.index(me) + s) % size] for s in range(size)] for me in range(size)]
    ids = jnp.asarray(table, jnp.int32)[lax.axis_index("tensor")]
    to_right = [(order[i], order[(i + 1) % size]) for i in range(size)]
    to_left = [(b, a) for a, b in to_right]

    def right_of(value):
        return lax.ppermute(value, "tensor", to_right)

    def left_of(value):
        return lax.ppermute(value, "tensor", to_left)

    own, slot = compact(routed, tokens, slots)

    right, left = right_of(own), left_of(own)
    sums = gate_up(ids, [0], [own], gate_weight, up_weight, None)
    for s in range(1, half):
        here = [right, left]
        if s + 1 < half:
            right, left = right_of(right), left_of(left)
        else:
            right, left = right_of(right[: slots // 2]), left_of(left[slots // 2 :])
        sums = gate_up(ids, [size - s, s], here, gate_weight, up_weight, sums)
    hidden = gate_up(ids, [half], [right, left], gate_weight, up_weight, sums, last=True)

    top, bottom = down(ids, [half], hidden, down_weight, width, split=True)
    right, left = right_of(top), left_of(bottom)
    for s in range(half - 1, 0, -1):
        ahead, behind = down(ids, [s, size - s], hidden, down_weight, width)
        if s == half - 1:
            rows = slots // 2
            ahead = jnp.concatenate([ahead[:rows] + right.astype(F32), ahead[rows:]])
            behind = jnp.concatenate([behind[:rows], behind[rows:] + left.astype(F32)])
        else:
            ahead = ahead + right.astype(F32)
            behind = behind + left.astype(F32)
        right, left = right_of(ahead.astype(BF16)), left_of(behind.astype(BF16))
    (mine,) = down(ids, [0], hidden, down_weight, width)

    slot = slot.reshape(-1)
    slot_ids = jnp.arange(slots, dtype=jnp.int32)
    place = (slot[:, None] == slot_ids[None, :]).astype(BF16)
    scale = jnp.sum(jnp.where(slot_ids[:, None] == slot[None, :], factor[None, :], 0.0), axis=1)
    return spread(place, scale[:, None], mine, right, left)


def plain_plan(slots, tokens, routed, factor, gate_weight, up_weight, down_weight):
    slot = jnp.where(routed, jnp.cumsum(routed.astype(jnp.int32)) - 1, -1)
    slot_ids = jnp.arange(slots, dtype=jnp.int32)
    select = slot_ids[:, None] == slot[None, :]
    chosen = dot(select.astype(BF16), tokens).astype(BF16)
    scale = jnp.sum(jnp.where(select, factor[None, :], 0.0), axis=1)
    full = lax.all_gather(chosen, "tensor", axis=1, tiled=True)
    gate, up = dot(full, gate_weight), dot(full, up_weight)
    hidden = (jax.nn.silu(gate) * up).astype(BF16)
    partial = dot(hidden, down_weight) * scale[:, None]
    total = lax.psum_scatter(partial, "tensor", scatter_dimension=1, tiled=True)
    return dot(select.T.astype(BF16), total.astype(BF16)).astype(BF16)


def local(size, tokens, expert_index, combine_weight, gate_weight, up_weight, down_weight):
    chosen = expert_index == 0
    routed = jnp.any(chosen, axis=1)
    factor = jnp.sum(jnp.where(chosen, combine_weight, 0.0), axis=1)
    rest = (tokens, routed, factor, gate_weight, up_weight, down_weight)
    fits = (
        size >= 4
        and size % 2 == 0
        and tokens.shape[1] % TILE == 0
        and gate_weight.shape[1] % TILE == 0
        and tokens.shape[0] % LANES == 0
    )
    if fits:
        return ring_plan(size, MOST, *rest)
    return plain_plan(MOST, *rest)


def solution(mesh):
    rows = P(("parts", "dp"), "tensor")
    in_specs = (
        rows,
        P(("parts", "dp"), None),
        P(("parts", "dp"), None),
        P(None, "tensor"),
        P(None, "tensor"),
        P("tensor", None),
    )
    return jax.shard_map(
        functools.partial(local, mesh.shape["tensor"]),
        mesh=mesh,
        in_specs=in_specs,
        out_specs=rows,
        check_vma=False,
    )
```

```python
import functools

import jax
import jax.numpy as jnp
from jax import lax
from jax.experimental import pallas as pl
from jax.experimental.pallas import tpu as pltpu
from jax.sharding import PartitionSpec as P

MOST = 512
LANES = 128
TILE = 256
WIDE = 512
COST = 2
F32 = jnp.float32
BF16 = jnp.bfloat16
VMEM_BYTES = 28 * 1024 * 1024


def params():
    return pltpu.CompilerParams(vmem_limit_bytes=VMEM_BYTES)


def dot(a, b):
    return jnp.dot(a, b, preferred_element_type=F32)


def compact_kernel(routed_ref, tokens_ref, chosen_ref, slot_ref, select_ref):
    slots = select_ref.shape[0]
    groups = routed_ref.shape[0]
    routed = routed_ref[...]
    above = lax.broadcasted_iota(jnp.int32, (LANES, LANES), 0) <= lax.broadcasted_iota(
        jnp.int32, (LANES, LANES), 1
    )
    within = dot(routed.astype(BF16), jnp.where(above, 1.0, 0.0).astype(BF16))
    before = jnp.zeros((1, 1), F32)
    slot_ids = lax.broadcasted_iota(jnp.int32, (slots, LANES), 0)
    for g in range(groups):
        row = within[g : g + 1, :] + before
        before = row[:, LANES - 1 :]
        slot = jnp.where(routed[g : g + 1, :] > 0, row.astype(jnp.int32) - 1, -1)
        slot_ref[g : g + 1, :] = slot
        select_ref[:, g * LANES : (g + 1) * LANES] = jnp.where(slot_ids == slot, 1.0, 0.0).astype(BF16)
    chosen_ref[...] = dot(select_ref[...], tokens_ref[...]).astype(BF16)


def compact(routed, tokens, slots):
    count, width = tokens.shape
    groups = count // LANES
    return pl.pallas_call(
        compact_kernel,
        out_shape=(
            jax.ShapeDtypeStruct((slots, width), BF16),
            jax.ShapeDtypeStruct((groups, LANES), jnp.int32),
        ),
        scratch_shapes=[pltpu.VMEM((slots, count), BF16)],
        compiler_params=params(),
        name="compact",
    )(routed.astype(F32).reshape(groups, LANES), tokens)


def silu(value):
    return value / (1.0 + jnp.exp(-value))


def gate_up_kernel(ids_ref, *refs, steps, pieces, first, last):
    xs, refs = refs[:pieces], refs[pieces:]
    gate_weight, up_weight, *refs = refs
    gate_in, up_in = (None, None) if first else refs[:2]
    refs = refs if first else refs[2:]
    hold, sem = refs[-2:]
    width = xs[0].shape[1]
    blocks, tile = hold.shape[0], hold.shape[-1]

    def copy(n, which, j):
        weight = (gate_weight, up_weight)[which]
        rows = pl.ds(pl.multiple_of(ids_ref[steps[j]] * width, width), width)
        return pltpu.make_async_copy(
            weight.at[rows, n * tile : (n + 1) * tile],
            hold.at[n, which, j * width : (j + 1) * width],
            sem.at[n, which, j],
        )

    for n in range(blocks):
        for which in range(2):
            for j in range(len(steps)):
                copy(n, which, j).start()
    if last:
        x = jnp.concatenate([piece[...] for piece in xs], axis=0)
    else:
        x = jnp.concatenate([piece[...] for piece in xs], axis=1)
    for n in range(blocks):
        at = slice(n * tile, (n + 1) * tile)
        values = []
        for which in range(2):
            for j in range(len(steps)):
                copy(n, which, j).wait()
            value = dot(x, hold[n, which])
            if not first:
                value = (gate_in, up_in)[which][:, at] + value
            values.append(value)
        if last:
            refs[0][:, at] = (silu(values[0]) * values[1]).astype(BF16)
        else:
            refs[0][:, at], refs[1][:, at] = values


def gate_up(ids, steps, xs, gate_weight, up_weight, sums, last=False):
    width = xs[0].shape[1]
    hidden = gate_weight.shape[1]
    slots = xs[0].shape[0] * (len(xs) if last else 1)
    first = sums is None
    on_chip = pl.BlockSpec(memory_space=pltpu.VMEM)
    away = pl.BlockSpec(memory_space=pl.ANY)
    operands = [*xs, gate_weight, up_weight, *([] if first else sums)]
    aliases = {}
    if last:
        out_shape, out_specs = jax.ShapeDtypeStruct((slots, hidden), BF16), on_chip
    else:
        out_shape = (pltpu.VMEM((slots, hidden), F32),) * 2
        out_specs = (on_chip, on_chip)
        if not first:
            at = 1 + len(operands) - 2
            aliases = {at: 0, at + 1: 1}
    blocks = hidden // WIDE
    flops = 4 * slots * width * hidden * len(steps)
    moved = 4 * width * hidden * len(steps)
    return pl.pallas_call(
        functools.partial(gate_up_kernel, steps=steps, pieces=len(xs), first=first, last=last),
        in_specs=[pl.BlockSpec(memory_space=pltpu.SMEM)]
        + [on_chip] * len(xs)
        + [away] * 2
        + [on_chip] * (0 if first else 2),
        out_specs=out_specs,
        out_shape=out_shape,
        scratch_shapes=[
            pltpu.VMEM((blocks, 2, width * len(steps), WIDE), BF16),
            pltpu.SemaphoreType.DMA((blocks, 2, len(steps))),
        ],
        input_output_aliases=aliases,
        compiler_params=params(),
        cost_estimate=pl.CostEstimate(flops=COST * flops, bytes_accessed=moved, transcendentals=0),
        name="gate_up",
    )(ids, *operands)


def down_kernel(ids_ref, hidden_ref, weight_ref, *refs, steps, split):
    outs, hold, sem = refs[:-2], *refs[-2:]
    width = hold.shape[-1]
    depth = hidden_ref.shape[1]
    cuts = sem.shape[1]
    deep = depth // cuts

    def copy(i, k):
        columns = pl.ds(pl.multiple_of(ids_ref[steps[i]] * width, width), width)
        rows = slice(k * deep, (k + 1) * deep)
        return pltpu.make_async_copy(weight_ref.at[rows, columns], hold.at[i, rows], sem.at[i, k])

    for i in range(len(steps)):
        for k in range(cuts):
            copy(i, k).start()
    for i in range(len(steps)):
        for n in range(width // TILE):
            at = slice(n * TILE, (n + 1) * TILE)
            if n == 0:
                value = None
                for k in range(cuts):
                    rows = slice(k * deep, (k + 1) * deep)
                    copy(i, k).wait()
                    term = dot(hidden_ref[:, rows], hold[i, rows, at])
                    value = term if value is None else value + term
            else:
                value = dot(hidden_ref[...], hold[i, :, at])
            if split:
                rows = outs[0].shape[0]
                outs[0][:, at] = value[:rows].astype(BF16)
                outs[1][:, at] = value[rows:].astype(BF16)
            else:
                outs[i][:, at] = value


def down(ids, steps, hidden, down_weight, width, split=False):
    slots, depth = hidden.shape
    if split:
        shape, kind, outs = (slots // 2, width), BF16, 2
    else:
        shape, kind, outs = (slots, width), F32, len(steps)
    on_chip = pl.BlockSpec(memory_space=pltpu.VMEM)
    return pl.pallas_call(
        functools.partial(down_kernel, steps=steps, split=split),
        in_specs=[pl.BlockSpec(memory_space=pltpu.SMEM), on_chip, pl.BlockSpec(memory_space=pl.ANY)],
        out_specs=(on_chip,) * outs,
        out_shape=(jax.ShapeDtypeStruct(shape, kind),) * outs,
        scratch_shapes=[
            pltpu.VMEM((len(steps), depth, width), BF16),
            pltpu.SemaphoreType.DMA((len(steps), 4)),
        ],
        compiler_params=params(),
        cost_estimate=pl.CostEstimate(
            flops=COST * 2 * slots * depth * width * len(steps),
            bytes_accessed=2 * depth * width * len(steps),
            transcendentals=0,
        ),
        name="down",
    )(ids, hidden, down_weight)


def spread_kernel(place_ref, scale_ref, own_ref, right_ref, left_ref, out_ref):
    total = own_ref[...] + right_ref[...].astype(F32) + left_ref[...].astype(F32)
    scaled = (total * scale_ref[...]).astype(BF16)
    out_ref[...] = dot(place_ref[...], scaled).astype(BF16)


def spread(place, scale, own, right, left):
    count, slots = place.shape
    width = own.shape[1]
    block = pl.BlockSpec((slots, TILE), lambda n: (0, n))
    return pl.pallas_call(
        spread_kernel,
        grid=(width // TILE,),
        in_specs=[
            pl.BlockSpec(place.shape, lambda n: (0, 0)),
            pl.BlockSpec(scale.shape, lambda n: (0, 0)),
            block,
            block,
            block,
        ],
        out_specs=pl.BlockSpec((count, TILE), lambda n: (0, n)),
        out_shape=jax.ShapeDtypeStruct((count, width), BF16),
        compiler_params=params(),
        name="spread",
    )(place, scale, own, right, left)


def ring_of(size):
    return [*range(0, size, 2), *range(size - 1, 0, -2)]


def ring_plan(size, slots, tokens, routed, factor, gate_weight, up_weight, down_weight):
    width = tokens.shape[1]
    half = size // 2
    order = ring_of(size)
    table = [[order[(order.index(me) + s) % size] for s in range(size)] for me in range(size)]
    ids = jnp.asarray(table, jnp.int32)[lax.axis_index("tensor")]
    to_right = [(order[i], order[(i + 1) % size]) for i in range(size)]
    to_left = [(b, a) for a, b in to_right]

    def right_of(value):
        return lax.ppermute(value, "tensor", to_right)

    def left_of(value):
        return lax.ppermute(value, "tensor", to_left)

    own, slot = compact(routed, tokens, slots)

    right, left = right_of(own), left_of(own)
    sums = gate_up(ids, [0], [own], gate_weight, up_weight, None)
    for s in range(1, half):
        here = [right, left]
        if s + 1 < half:
            right, left = right_of(right), left_of(left)
        else:
            right, left = right_of(right[: slots // 2]), left_of(left[slots // 2 :])
        sums = gate_up(ids, [size - s, s], here, gate_weight, up_weight, sums)
    hidden = gate_up(ids, [half], [right, left], gate_weight, up_weight, sums, last=True)

    top, bottom = down(ids, [half], hidden, down_weight, width, split=True)
    right, left = right_of(top), left_of(bottom)
    for s in range(half - 1, 0, -1):
        ahead, behind = down(ids, [s, size - s], hidden, down_weight, width)
        if s == half - 1:
            rows = slots // 2
            ahead = jnp.concatenate([ahead[:rows] + right.astype(F32), ahead[rows:]])
            behind = jnp.concatenate([behind[:rows], behind[rows:] + left.astype(F32)])
        else:
            ahead = ahead + right.astype(F32)
            behind = behind + left.astype(F32)
        right, left = right_of(ahead.astype(BF16)), left_of(behind.astype(BF16))
    (mine,) = down(ids, [0], hidden, down_weight, width)

    slot = slot.reshape(-1)
    slot_ids = jnp.arange(slots, dtype=jnp.int32)
    place = (slot[:, None] == slot_ids[None, :]).astype(BF16)
    scale = jnp.sum(jnp.where(slot_ids[:, None] == slot[None, :], factor[None, :], 0.0), axis=1)
    return spread(place, scale[:, None], mine, right, left)


def plain_plan(slots, tokens, routed, factor, gate_weight, up_weight, down_weight):
    slot = jnp.where(routed, jnp.cumsum(routed.astype(jnp.int32)) - 1, -1)
    slot_ids = jnp.arange(slots, dtype=jnp.int32)
    select = slot_ids[:, None] == slot[None, :]
    chosen = dot(select.astype(BF16), tokens).astype(BF16)
    scale = jnp.sum(jnp.where(select, factor[None, :], 0.0), axis=1)
    full = lax.all_gather(chosen, "tensor", axis=1, tiled=True)
    gate, up = dot(full, gate_weight), dot(full, up_weight)
    hidden = (jax.nn.silu(gate) * up).astype(BF16)
    partial = dot(hidden, down_weight) * scale[:, None]
    total = lax.psum_scatter(partial, "tensor", scatter_dimension=1, tiled=True)
    return dot(select.T.astype(BF16), total.astype(BF16)).astype(BF16)


def local(size, tokens, expert_index, combine_weight, gate_weight, up_weight, down_weight):
    chosen = expert_index == 0
    routed = jnp.any(chosen, axis=1)
    factor = jnp.sum(jnp.where(chosen, combine_weight, 0.0), axis=1)
    rest = (tokens, routed, factor, gate_weight, up_weight, down_weight)
    fits = (
        size >= 4
        and size % 2 == 0
        and tokens.shape[1] % TILE == 0
        and gate_weight.shape[1] % WIDE == 0
        and tokens.shape[0] % LANES == 0
    )
    if fits:
        return ring_plan(size, MOST, *rest)
    return plain_plan(MOST, *rest)


def solution(mesh):
    rows = P(("parts", "dp"), "tensor")
    in_specs = (
        rows,
        P(("parts", "dp"), None),
        P(("parts", "dp"), None),
        P(None, "tensor"),
        P(None, "tensor"),
        P("tensor", None),
    )
    return jax.shard_map(
        functools.partial(local, mesh.shape["tensor"]),
        mesh=mesh,
        in_specs=in_specs,
        out_specs=rows,
        check_vma=False,
    )
```

```python
import functools

import jax
import jax.numpy as jnp
from jax import lax
from jax.experimental import pallas as pl
from jax.experimental.pallas import tpu as pltpu
from jax.sharding import PartitionSpec as P

MOST = 512
LANES = 128
TILE = 256
WIDE = 512
COST = 2
F32 = jnp.float32
BF16 = jnp.bfloat16
VMEM_BYTES = 28 * 1024 * 1024


def params():
    return pltpu.CompilerParams(vmem_limit_bytes=VMEM_BYTES)


def dot(a, b):
    return jnp.dot(a, b, preferred_element_type=F32)


def compact_kernel(routed_ref, tokens_ref, chosen_ref, slot_ref, select_ref):
    slots = select_ref.shape[0]
    groups = routed_ref.shape[0]
    routed = routed_ref[...]
    above = lax.broadcasted_iota(jnp.int32, (LANES, LANES), 0) <= lax.broadcasted_iota(
        jnp.int32, (LANES, LANES), 1
    )
    within = dot(routed.astype(BF16), jnp.where(above, 1.0, 0.0).astype(BF16))
    before = jnp.zeros((1, 1), F32)
    slot_ids = lax.broadcasted_iota(jnp.int32, (slots, LANES), 0)
    for g in range(groups):
        row = within[g : g + 1, :] + before
        before = row[:, LANES - 1 :]
        slot = jnp.where(routed[g : g + 1, :] > 0, row.astype(jnp.int32) - 1, -1)
        slot_ref[g : g + 1, :] = slot
        select_ref[:, g * LANES : (g + 1) * LANES] = jnp.where(slot_ids == slot, 1.0, 0.0).astype(BF16)
    chosen_ref[...] = dot(select_ref[...], tokens_ref[...]).astype(BF16)


def compact(routed, tokens, slots):
    count, width = tokens.shape
    groups = count // LANES
    return pl.pallas_call(
        compact_kernel,
        out_shape=(
            jax.ShapeDtypeStruct((slots, width), BF16),
            jax.ShapeDtypeStruct((groups, LANES), jnp.int32),
        ),
        scratch_shapes=[pltpu.VMEM((slots, count), BF16)],
        compiler_params=params(),
        name="compact",
    )(routed.astype(F32).reshape(groups, LANES), tokens)


def silu(value):
    return value / (1.0 + jnp.exp(-value))


def gate_up_kernel(ids_ref, *refs, steps, pieces, first, last):
    xs, refs = refs[:pieces], refs[pieces:]
    gate_weight, up_weight, *refs = refs
    gate_in, up_in = (None, None) if first else refs[:2]
    refs = refs if first else refs[2:]
    hold, sem = refs[-2:]
    width = xs[0].shape[1]
    blocks, tile = hold.shape[0], hold.shape[-1]

    def copy(n, which, j):
        weight = (gate_weight, up_weight)[which]
        rows = pl.ds(pl.multiple_of(ids_ref[steps[j]] * width, width), width)
        columns = pl.ds(pl.multiple_of(n * tile, tile), tile)
        return pltpu.make_async_copy(
            weight.at[rows, columns],
            hold.at[n, which, j * width : (j + 1) * width],
            sem.at[n, which, j],
        )

    def begin(n, carry):
        for which in range(2):
            for j in range(len(steps)):
                copy(n, which, j).start()
        return carry

    def block(n, carry):
        at = pl.ds(pl.multiple_of(n * tile, tile), tile)
        x = jnp.concatenate([piece[...] for piece in xs], axis=0 if last else 1)
        values = []
        for which in range(2):
            for j in range(len(steps)):
                copy(n, which, j).wait()
            value = dot(x, hold[n, which])
            if not first:
                value = (gate_in, up_in)[which][:, at] + value
            values.append(value)
        if last:
            refs[0][:, at] = (silu(values[0]) * values[1]).astype(BF16)
        else:
            refs[0][:, at], refs[1][:, at] = values
        return carry

    lax.fori_loop(0, blocks, begin, 0)
    lax.fori_loop(0, blocks, block, 0)


def gate_up(ids, steps, xs, gate_weight, up_weight, sums, last=False):
    width = xs[0].shape[1]
    hidden = gate_weight.shape[1]
    slots = xs[0].shape[0] * (len(xs) if last else 1)
    first = sums is None
    on_chip = pl.BlockSpec(memory_space=pltpu.VMEM)
    away = pl.BlockSpec(memory_space=pl.ANY)
    operands = [*xs, gate_weight, up_weight, *([] if first else sums)]
    aliases = {}
    if last:
        out_shape, out_specs = jax.ShapeDtypeStruct((slots, hidden), BF16), on_chip
    else:
        out_shape = (pltpu.VMEM((slots, hidden), F32),) * 2
        out_specs = (on_chip, on_chip)
        if not first:
            at = 1 + len(operands) - 2
            aliases = {at: 0, at + 1: 1}
    blocks = hidden // WIDE
    flops = 4 * slots * width * hidden * len(steps)
    moved = 4 * width * hidden * len(steps)
    return pl.pallas_call(
        functools.partial(gate_up_kernel, steps=steps, pieces=len(xs), first=first, last=last),
        in_specs=[pl.BlockSpec(memory_space=pltpu.SMEM)]
        + [on_chip] * len(xs)
        + [away] * 2
        + [on_chip] * (0 if first else 2),
        out_specs=out_specs,
        out_shape=out_shape,
        scratch_shapes=[
            pltpu.VMEM((blocks, 2, width * len(steps), WIDE), BF16),
            pltpu.SemaphoreType.DMA((blocks, 2, len(steps))),
        ],
        input_output_aliases=aliases,
        compiler_params=params(),
        cost_estimate=pl.CostEstimate(flops=COST * flops, bytes_accessed=moved, transcendentals=0),
        name="gate_up",
    )(ids, *operands)


def down_kernel(ids_ref, hidden_ref, weight_ref, *refs, steps, split):
    outs, hold, sem = refs[:-2], *refs[-2:]
    width = hold.shape[-1]
    depth = hidden_ref.shape[1]
    cuts = sem.shape[1]
    deep = depth // cuts

    def copy(i, k):
        columns = pl.ds(pl.multiple_of(ids_ref[steps[i]] * width, width), width)
        rows = slice(k * deep, (k + 1) * deep)
        return pltpu.make_async_copy(weight_ref.at[rows, columns], hold.at[i, rows], sem.at[i, k])

    for i in range(len(steps)):
        for k in range(cuts):
            copy(i, k).start()
    for i in range(len(steps)):

        def block(n, carry, i=i):
            @pl.when(n == 0)
            def _():
                for k in range(cuts):
                    copy(i, k).wait()

            at = pl.ds(pl.multiple_of(n * TILE, TILE), TILE)
            value = dot(hidden_ref[...], hold[i, :, at])
            if split:
                rows = outs[0].shape[0]
                outs[0][:, at] = value[:rows].astype(BF16)
                outs[1][:, at] = value[rows:].astype(BF16)
            else:
                outs[i][:, at] = value
            return carry

        lax.fori_loop(0, width // TILE, block, 0)


def down(ids, steps, hidden, down_weight, width, split=False):
    slots, depth = hidden.shape
    if split:
        shape, kind, outs = (slots // 2, width), BF16, 2
    else:
        shape, kind, outs = (slots, width), F32, len(steps)
    on_chip = pl.BlockSpec(memory_space=pltpu.VMEM)
    return pl.pallas_call(
        functools.partial(down_kernel, steps=steps, split=split),
        in_specs=[pl.BlockSpec(memory_space=pltpu.SMEM), on_chip, pl.BlockSpec(memory_space=pl.ANY)],
        out_specs=(on_chip,) * outs,
        out_shape=(jax.ShapeDtypeStruct(shape, kind),) * outs,
        scratch_shapes=[
            pltpu.VMEM((len(steps), depth, width), BF16),
            pltpu.SemaphoreType.DMA((len(steps), 4)),
        ],
        compiler_params=params(),
        cost_estimate=pl.CostEstimate(
            flops=COST * 2 * slots * depth * width * len(steps),
            bytes_accessed=2 * depth * width * len(steps),
            transcendentals=0,
        ),
        name="down",
    )(ids, hidden, down_weight)


def spread_kernel(place_ref, scale_ref, own_ref, right_ref, left_ref, out_ref):
    total = own_ref[...] + right_ref[...].astype(F32) + left_ref[...].astype(F32)
    scaled = (total * scale_ref[...]).astype(BF16)
    out_ref[...] = dot(place_ref[...], scaled).astype(BF16)


def spread(place, scale, own, right, left):
    count, slots = place.shape
    width = own.shape[1]
    block = pl.BlockSpec((slots, TILE), lambda n: (0, n))
    return pl.pallas_call(
        spread_kernel,
        grid=(width // TILE,),
        in_specs=[
            pl.BlockSpec(place.shape, lambda n: (0, 0)),
            pl.BlockSpec(scale.shape, lambda n: (0, 0)),
            block,
            block,
            block,
        ],
        out_specs=pl.BlockSpec((count, TILE), lambda n: (0, n)),
        out_shape=jax.ShapeDtypeStruct((count, width), BF16),
        compiler_params=params(),
        name="spread",
    )(place, scale, own, right, left)


def ring_of(size):
    return [*range(0, size, 2), *range(size - 1, 0, -2)]


def ring_plan(size, slots, tokens, routed, factor, gate_weight, up_weight, down_weight):
    width = tokens.shape[1]
    half = size // 2
    order = ring_of(size)
    table = [[order[(order.index(me) + s) % size] for s in range(size)] for me in range(size)]
    ids = jnp.asarray(table, jnp.int32)[lax.axis_index("tensor")]
    to_right = [(order[i], order[(i + 1) % size]) for i in range(size)]
    to_left = [(b, a) for a, b in to_right]

    def right_of(value):
        return lax.ppermute(value, "tensor", to_right)

    def left_of(value):
        return lax.ppermute(value, "tensor", to_left)

    own, slot = compact(routed, tokens, slots)

    right, left = right_of(own), left_of(own)
    sums = gate_up(ids, [0], [own], gate_weight, up_weight, None)
    for s in range(1, half):
        here = [right, left]
        if s + 1 < half:
            right, left = right_of(right), left_of(left)
        else:
            right, left = right_of(right[: slots // 2]), left_of(left[slots // 2 :])
        sums = gate_up(ids, [size - s, s], here, gate_weight, up_weight, sums)
    hidden = gate_up(ids, [half], [right, left], gate_weight, up_weight, sums, last=True)

    top, bottom = down(ids, [half], hidden, down_weight, width, split=True)
    right, left = right_of(top), left_of(bottom)
    for s in range(half - 1, 0, -1):
        ahead, behind = down(ids, [s, size - s], hidden, down_weight, width)
        if s == half - 1:
            rows = slots // 2
            ahead = jnp.concatenate([ahead[:rows] + right.astype(F32), ahead[rows:]])
            behind = jnp.concatenate([behind[:rows], behind[rows:] + left.astype(F32)])
        else:
            ahead = ahead + right.astype(F32)
            behind = behind + left.astype(F32)
        right, left = right_of(ahead.astype(BF16)), left_of(behind.astype(BF16))
    (mine,) = down(ids, [0], hidden, down_weight, width)

    slot = slot.reshape(-1)
    slot_ids = jnp.arange(slots, dtype=jnp.int32)
    place = (slot[:, None] == slot_ids[None, :]).astype(BF16)
    scale = jnp.sum(jnp.where(slot_ids[:, None] == slot[None, :], factor[None, :], 0.0), axis=1)
    return spread(place, scale[:, None], mine, right, left)


def plain_plan(slots, tokens, routed, factor, gate_weight, up_weight, down_weight):
    slot = jnp.where(routed, jnp.cumsum(routed.astype(jnp.int32)) - 1, -1)
    slot_ids = jnp.arange(slots, dtype=jnp.int32)
    select = slot_ids[:, None] == slot[None, :]
    chosen = dot(select.astype(BF16), tokens).astype(BF16)
    scale = jnp.sum(jnp.where(select, factor[None, :], 0.0), axis=1)
    full = lax.all_gather(chosen, "tensor", axis=1, tiled=True)
    gate, up = dot(full, gate_weight), dot(full, up_weight)
    hidden = (jax.nn.silu(gate) * up).astype(BF16)
    partial = dot(hidden, down_weight) * scale[:, None]
    total = lax.psum_scatter(partial, "tensor", scatter_dimension=1, tiled=True)
    return dot(select.T.astype(BF16), total.astype(BF16)).astype(BF16)


def local(size, tokens, expert_index, combine_weight, gate_weight, up_weight, down_weight):
    chosen = expert_index == 0
    routed = jnp.any(chosen, axis=1)
    factor = jnp.sum(jnp.where(chosen, combine_weight, 0.0), axis=1)
    rest = (tokens, routed, factor, gate_weight, up_weight, down_weight)
    fits = (
        size >= 4
        and size % 2 == 0
        and tokens.shape[1] % TILE == 0
        and gate_weight.shape[1] % WIDE == 0
        and tokens.shape[0] % LANES == 0
    )
    if not fits:
        return plain_plan(MOST, *rest)
    return ring_plan(size, MOST, *rest)


def solution(mesh):
    rows = P(("parts", "dp"), "tensor")
    in_specs = (
        rows,
        P(("parts", "dp"), None),
        P(("parts", "dp"), None),
        P(None, "tensor"),
        P(None, "tensor"),
        P("tensor", None),
    )
    return jax.shard_map(
        functools.partial(local, mesh.shape["tensor"]),
        mesh=mesh,
        in_specs=in_specs,
        out_specs=rows,
        check_vma=False,
    )
```

```python
import functools

import jax
import jax.numpy as jnp
from jax import lax
from jax.experimental import pallas as pl
from jax.experimental.pallas import tpu as pltpu
from jax.sharding import PartitionSpec as P

MOST = 512
LANES = 128
TILE = 256
WIDE = 512
COST = 2
F32 = jnp.float32
BF16 = jnp.bfloat16
VMEM_BYTES = 28 * 1024 * 1024


def params():
    return pltpu.CompilerParams(vmem_limit_bytes=VMEM_BYTES)


def dot(a, b):
    return jnp.dot(a, b, preferred_element_type=F32)


def compact_kernel(routed_ref, tokens_ref, chosen_ref, slot_ref, select_ref):
    slots = select_ref.shape[0]
    groups = routed_ref.shape[0]
    routed = routed_ref[...]
    above = lax.broadcasted_iota(jnp.int32, (LANES, LANES), 0) <= lax.broadcasted_iota(
        jnp.int32, (LANES, LANES), 1
    )
    within = dot(routed.astype(BF16), jnp.where(above, 1.0, 0.0).astype(BF16))
    before = jnp.zeros((1, 1), F32)
    slot_ids = lax.broadcasted_iota(jnp.int32, (slots, LANES), 0)
    for g in range(groups):
        row = within[g : g + 1, :] + before
        before = row[:, LANES - 1 :]
        slot = jnp.where(routed[g : g + 1, :] > 0, row.astype(jnp.int32) - 1, -1)
        slot_ref[g : g + 1, :] = slot
        select_ref[:, g * LANES : (g + 1) * LANES] = jnp.where(slot_ids == slot, 1.0, 0.0).astype(BF16)
    chosen_ref[...] = dot(select_ref[...], tokens_ref[...]).astype(BF16)


def compact(routed, tokens, slots):
    count, width = tokens.shape
    groups = count // LANES
    return pl.pallas_call(
        compact_kernel,
        out_shape=(
            jax.ShapeDtypeStruct((slots, width), BF16),
            jax.ShapeDtypeStruct((groups, LANES), jnp.int32),
        ),
        scratch_shapes=[pltpu.VMEM((slots, count), BF16)],
        compiler_params=params(),
        name="compact",
    )(routed.astype(F32).reshape(groups, LANES), tokens)


def silu(value):
    return value / (1.0 + jnp.exp(-value))


def gate_up_kernel(ids_ref, *refs, steps, first, fetch):
    xs, refs = refs[: len(steps)], refs[len(steps) :]
    gate_weight, up_weight, *refs = refs
    down_weight, refs = (refs[0], refs[1:]) if fetch is not None else (None, refs)
    gate_in, up_in = (None, None) if first else refs[:2]
    refs = refs if first else refs[2:]
    gate_out, up_out, *refs = refs
    hold, sem = refs[-2 if fetch is None else -4 :][:2]
    width = xs[0].shape[1]
    blocks, tile = hold.shape[0], hold.shape[-1]

    def copy(n, which, step, into, signal):
        rows = pl.ds(pl.multiple_of(ids_ref[step] * width, width), width)
        columns = pl.ds(pl.multiple_of(n * tile, tile), tile)
        weight = (gate_weight, up_weight)[which]
        return pltpu.make_async_copy(weight.at[rows, columns], into, signal)

    def mine(n, which, j):
        into = hold.at[n, which, j * width : (j + 1) * width]
        return copy(n, which, steps[j], into, sem.at[n, which, j])

    def begin(n, carry):
        for which in range(2):
            for j in range(len(steps)):
                mine(n, which, j).start()
        return carry

    def block(n, carry):
        at = pl.ds(pl.multiple_of(n * tile, tile), tile)
        x = jnp.concatenate([piece[...] for piece in xs], axis=1)
        for which in range(2):
            for j in range(len(steps)):
                mine(n, which, j).wait()
            value = dot(x, hold[n, which])
            if not first:
                value = (gate_in, up_in)[which][:, at] + value
            (gate_out, up_out)[which][:, at] = value
        return carry

    lax.fori_loop(0, blocks, begin, 0)
    if fetch is None:
        lax.fori_loop(0, blocks, block, 0)
        return

    next_ref, down_ref, _, _, next_sem, down_sem = refs
    depth, breadth = down_ref.shape
    columns = pl.ds(pl.multiple_of(ids_ref[fetch] * breadth, breadth), breadth)
    below = pltpu.make_async_copy(down_weight.at[:, columns], down_ref, down_sem)

    def ahead(n, which):
        return copy(n, which, fetch, next_ref.at[n, which], next_sem.at[n, which])

    def begin_ahead(n, carry):
        for which in range(2):
            ahead(n, which).start()
        return carry

    def end_ahead(n, carry):
        for which in range(2):
            ahead(n, which).wait()
        return carry

    lax.fori_loop(0, blocks, begin_ahead, 0)
    below.start()
    lax.fori_loop(0, blocks, block, 0)
    lax.fori_loop(0, blocks, end_ahead, 0)
    below.wait()


def gate_up(ids, steps, xs, gate_weight, up_weight, sums, down_weight=None, fetch=None):
    slots, width = xs[0].shape
    hidden = gate_weight.shape[1]
    first = sums is None
    on_chip = pl.BlockSpec(memory_space=pltpu.VMEM)
    away = pl.BlockSpec(memory_space=pl.ANY)
    weights = [gate_weight, up_weight] + ([] if fetch is None else [down_weight])
    operands = [*xs, *weights, *([] if first else sums)]
    at = 1 + len(operands) - 2
    blocks = hidden // WIDE
    out_shape = [pltpu.VMEM((slots, hidden), F32)] * 2
    scratch = [
        pltpu.VMEM((blocks, 2, width * len(steps), WIDE), BF16),
        pltpu.SemaphoreType.DMA((blocks, 2, len(steps))),
    ]
    if fetch is not None:
        out_shape += [pltpu.VMEM((blocks, 2, width, WIDE), BF16), pltpu.VMEM((hidden, width), BF16)]
        scratch += [pltpu.SemaphoreType.DMA((blocks, 2)), pltpu.SemaphoreType.DMA]
    flops = 4 * slots * width * hidden * len(steps)
    moved = 4 * width * hidden * len(steps)
    return pl.pallas_call(
        functools.partial(gate_up_kernel, steps=steps, first=first, fetch=fetch),
        in_specs=[pl.BlockSpec(memory_space=pltpu.SMEM)]
        + [on_chip] * len(xs)
        + [away] * len(weights)
        + [on_chip] * (0 if first else 2),
        out_specs=[on_chip] * len(out_shape),
        out_shape=out_shape,
        scratch_shapes=scratch,
        input_output_aliases={} if first else {at: 0, at + 1: 1},
        compiler_params=params(),
        cost_estimate=pl.CostEstimate(flops=COST * flops, bytes_accessed=moved, transcendentals=0),
        name="gate_up",
    )(ids, *operands)


def turn_kernel(top_x, bottom_x, gate_in, up_in, next_ref, down_ref, hidden_ref, top_out, bottom_out):
    blocks, tile = next_ref.shape[0], next_ref.shape[-1]
    rows = top_out.shape[0]

    def block(n, carry):
        at = pl.ds(pl.multiple_of(n * tile, tile), tile)
        x = jnp.concatenate([top_x[...], bottom_x[...]], axis=0)
        gate = gate_in[:, at] + dot(x, next_ref[n, 0])
        up = up_in[:, at] + dot(x, next_ref[n, 1])
        hidden_ref[:, at] = (silu(gate) * up).astype(BF16)
        return carry

    def leave(n, carry):
        at = pl.ds(pl.multiple_of(n * TILE, TILE), TILE)
        value = dot(hidden_ref[...], down_ref[:, at])
        top_out[:, at] = value[:rows].astype(BF16)
        bottom_out[:, at] = value[rows:].astype(BF16)
        return carry

    lax.fori_loop(0, blocks, block, 0)
    lax.fori_loop(0, down_ref.shape[1] // TILE, leave, 0)


def turn(top, bottom, sums, next_weights, next_down):
    rows, width = top.shape
    hidden = sums[0].shape[1]
    on_chip = pl.BlockSpec(memory_space=pltpu.VMEM)
    return pl.pallas_call(
        turn_kernel,
        in_specs=[on_chip] * 6,
        out_specs=[on_chip] * 3,
        out_shape=[
            pltpu.VMEM((2 * rows, hidden), BF16),
            jax.ShapeDtypeStruct((rows, width), BF16),
            jax.ShapeDtypeStruct((rows, width), BF16),
        ],
        compiler_params=params(),
        cost_estimate=pl.CostEstimate(
            flops=12 * rows * width * hidden, bytes_accessed=0, transcendentals=0
        ),
        name="turn",
    )(top, bottom, *sums, next_weights, next_down)


def down_kernel(ids_ref, hidden_ref, weight_ref, *refs, steps):
    outs, hold, sem = refs[:-2], *refs[-2:]
    width = hold.shape[-1]
    depth = hidden_ref.shape[1]
    cuts = sem.shape[1]
    deep = depth // cuts

    def copy(i, k):
        columns = pl.ds(pl.multiple_of(ids_ref[steps[i]] * width, width), width)
        rows = slice(k * deep, (k + 1) * deep)
        return pltpu.make_async_copy(weight_ref.at[rows, columns], hold.at[i, rows], sem.at[i, k])

    for i in range(len(steps)):
        for k in range(cuts):
            copy(i, k).start()
    for i in range(len(steps)):

        def block(n, carry, i=i):
            @pl.when(n == 0)
            def _():
                for k in range(cuts):
                    copy(i, k).wait()

            at = pl.ds(pl.multiple_of(n * TILE, TILE), TILE)
            outs[i][:, at] = dot(hidden_ref[...], hold[i, :, at])
            return carry

        lax.fori_loop(0, width // TILE, block, 0)


def down(ids, steps, hidden, down_weight, width):
    slots, depth = hidden.shape
    on_chip = pl.BlockSpec(memory_space=pltpu.VMEM)
    return pl.pallas_call(
        functools.partial(down_kernel, steps=steps),
        in_specs=[pl.BlockSpec(memory_space=pltpu.SMEM), on_chip, pl.BlockSpec(memory_space=pl.ANY)],
        out_specs=(on_chip,) * len(steps),
        out_shape=(jax.ShapeDtypeStruct((slots, width), F32),) * len(steps),
        scratch_shapes=[
            pltpu.VMEM((len(steps), depth, width), BF16),
            pltpu.SemaphoreType.DMA((len(steps), 4)),
        ],
        compiler_params=params(),
        cost_estimate=pl.CostEstimate(
            flops=COST * 2 * slots * depth * width * len(steps),
            bytes_accessed=2 * depth * width * len(steps),
            transcendentals=0,
        ),
        name="down",
    )(ids, hidden, down_weight)


def spread_kernel(place_ref, scale_ref, own_ref, right_ref, left_ref, out_ref):
    at = pl.ds(pl.multiple_of(pl.program_id(0) * TILE, TILE), TILE)
    total = own_ref[:, at] + right_ref[:, at].astype(F32) + left_ref[:, at].astype(F32)
    out_ref[...] = dot(place_ref[...], (total * scale_ref[...]).astype(BF16)).astype(BF16)


def spread(place, scale, own, right, left):
    count = place.shape[0]
    width = own.shape[1]
    return pl.pallas_call(
        spread_kernel,
        grid=(width // TILE,),
        in_specs=[pl.BlockSpec(memory_space=pltpu.VMEM)] * 5,
        out_specs=pl.BlockSpec((count, TILE), lambda n: (0, n)),
        out_shape=jax.ShapeDtypeStruct((count, width), BF16),
        compiler_params=params(),
        name="spread",
    )(place, scale, own, right, left)


def ring_of(size):
    return [*range(0, size, 2), *range(size - 1, 0, -2)]


def ring_plan(size, slots, tokens, routed, factor, gate_weight, up_weight, down_weight):
    width = tokens.shape[1]
    half = size // 2
    order = ring_of(size)
    table = [[order[(order.index(me) + s) % size] for s in range(size)] for me in range(size)]
    ids = jnp.asarray(table, jnp.int32)[lax.axis_index("tensor")]
    to_right = [(order[i], order[(i + 1) % size]) for i in range(size)]
    to_left = [(b, a) for a, b in to_right]

    def right_of(value):
        return lax.ppermute(value, "tensor", to_right)

    def left_of(value):
        return lax.ppermute(value, "tensor", to_left)

    def both(one, other):
        return lax.optimization_barrier((one, other))

    own, slot = compact(routed, tokens, slots)

    right, left = right_of(own), left_of(own)
    sums = gate_up(ids, [0], [own], gate_weight, up_weight, None)
    for s in range(1, half):
        here = [right, left]
        if s + 1 < half:
            right, left = right_of(right), left_of(left)
        else:
            right, left = right_of(right[: slots // 2]), left_of(left[slots // 2 :])
        if s == max(1, half - 2):
            *sums, next_weights, next_down = gate_up(
                ids, [size - s, s], here, gate_weight, up_weight, sums, down_weight, fetch=half
            )
        else:
            sums = gate_up(ids, [size - s, s], here, gate_weight, up_weight, sums)
    hidden, top, bottom = turn(right, left, sums, next_weights, next_down)

    right, left = both(right_of(top), left_of(bottom))
    for s in range(half - 1, 0, -1):
        ahead, behind = down(ids, [s, size - s], hidden, down_weight, width)
        if s == half - 1:
            rows = slots // 2
            ahead = jnp.concatenate([ahead[:rows] + right.astype(F32), ahead[rows:]])
            behind = jnp.concatenate([behind[:rows], behind[rows:] + left.astype(F32)])
        else:
            ahead = ahead + right.astype(F32)
            behind = behind + left.astype(F32)
        right, left = both(right_of(ahead.astype(BF16)), left_of(behind.astype(BF16)))
    (mine,) = down(ids, [0], hidden, down_weight, width)

    slot = slot.reshape(-1)
    slot_ids = jnp.arange(slots, dtype=jnp.int32)
    place = (slot[:, None] == slot_ids[None, :]).astype(BF16)
    scale = jnp.sum(jnp.where(slot_ids[:, None] == slot[None, :], factor[None, :], 0.0), axis=1)
    return spread(place, scale[:, None], mine, right, left)


def plain_plan(slots, tokens, routed, factor, gate_weight, up_weight, down_weight):
    slot = jnp.where(routed, jnp.cumsum(routed.astype(jnp.int32)) - 1, -1)
    slot_ids = jnp.arange(slots, dtype=jnp.int32)
    select = slot_ids[:, None] == slot[None, :]
    chosen = dot(select.astype(BF16), tokens).astype(BF16)
    scale = jnp.sum(jnp.where(select, factor[None, :], 0.0), axis=1)
    full = lax.all_gather(chosen, "tensor", axis=1, tiled=True)
    gate, up = dot(full, gate_weight), dot(full, up_weight)
    hidden = (jax.nn.silu(gate) * up).astype(BF16)
    partial = dot(hidden, down_weight) * scale[:, None]
    total = lax.psum_scatter(partial, "tensor", scatter_dimension=1, tiled=True)
    return dot(select.T.astype(BF16), total.astype(BF16)).astype(BF16)


def local(size, tokens, expert_index, combine_weight, gate_weight, up_weight, down_weight):
    chosen = expert_index == 0
    routed = jnp.any(chosen, axis=1)
    factor = jnp.sum(jnp.where(chosen, combine_weight, 0.0), axis=1)
    rest = (tokens, routed, factor, gate_weight, up_weight, down_weight)
    fits = (
        size >= 4
        and size % 2 == 0
        and tokens.shape[1] % TILE == 0
        and gate_weight.shape[1] % WIDE == 0
        and tokens.shape[0] % LANES == 0
    )
    if not fits:
        return plain_plan(MOST, *rest)
    return ring_plan(size, MOST, *rest)


def solution(mesh):
    rows = P(("parts", "dp"), "tensor")
    in_specs = (
        rows,
        P(("parts", "dp"), None),
        P(("parts", "dp"), None),
        P(None, "tensor"),
        P(None, "tensor"),
        P("tensor", None),
    )
    return jax.shard_map(
        functools.partial(local, mesh.shape["tensor"]),
        mesh=mesh,
        in_specs=in_specs,
        out_specs=rows,
        check_vma=False,
    )
```

```python
import functools

import jax
import jax.numpy as jnp
from jax import lax
from jax.experimental import pallas as pl
from jax.experimental.pallas import tpu as pltpu
from jax.sharding import PartitionSpec as P

MOST = 512
LANES = 128
TILE = 256
WIDE = 512
COST = 2
AHEAD = 4
F32 = jnp.float32
BF16 = jnp.bfloat16
VMEM_BYTES = 28 * 1024 * 1024


def params():
    return pltpu.CompilerParams(vmem_limit_bytes=VMEM_BYTES)


def dot(a, b):
    return jnp.dot(a, b, preferred_element_type=F32)


def compact_kernel(named_ref, tokens_ref, chosen_ref, slot_ref, select_ref, held_ref, sem):
    slots, count = select_ref.shape
    groups = count // LANES
    cuts = sem.shape[0]
    deep = count // cuts

    def bring(k):
        rows = slice(k * deep, (k + 1) * deep)
        return pltpu.make_async_copy(tokens_ref.at[rows], held_ref.at[rows], sem.at[k])

    for k in range(cuts):
        bring(k).start()
    hits = jnp.max(jnp.where(named_ref[...] == 0, 1.0, 0.0), axis=0, keepdims=True)
    routed = jnp.concatenate([hits[:, g * LANES : (g + 1) * LANES] for g in range(groups)], axis=0)
    above = lax.broadcasted_iota(jnp.int32, (LANES, LANES), 0) <= lax.broadcasted_iota(
        jnp.int32, (LANES, LANES), 1
    )
    within = dot(routed.astype(BF16), jnp.where(above, 1.0, 0.0).astype(BF16))
    before = jnp.zeros((1, 1), F32)
    slot_ids = lax.broadcasted_iota(jnp.int32, (slots, LANES), 0)
    for g in range(groups):
        row = within[g : g + 1, :] + before
        before = row[:, LANES - 1 :]
        slot = jnp.where(routed[g : g + 1, :] > 0, row.astype(jnp.int32) - 1, -1)
        slot_ref[g : g + 1, :] = slot
        select_ref[:, g * LANES : (g + 1) * LANES] = jnp.where(slot_ids == slot, 1.0, 0.0).astype(BF16)
    for k in range(cuts):
        bring(k).wait()
    chosen_ref[...] = dot(select_ref[...], held_ref[...]).astype(BF16)


def compact(expert_index, tokens, slots):
    count, width = tokens.shape
    groups = count // LANES
    return pl.pallas_call(
        compact_kernel,
        out_shape=(
            jax.ShapeDtypeStruct((slots, width), BF16),
            jax.ShapeDtypeStruct((groups, LANES), jnp.int32),
        ),
        in_specs=[pl.BlockSpec(memory_space=pltpu.VMEM), pl.BlockSpec(memory_space=pl.ANY)],
        scratch_shapes=[
            pltpu.VMEM((slots, count), BF16),
            pltpu.VMEM((count, width), BF16),
            pltpu.SemaphoreType.DMA((4,)),
        ],
        compiler_params=params(),
        name="compact",
    )(expert_index.T, pltpu.with_memory_space_constraint(tokens, pltpu.HBM))


def silu(value):
    return value / (1.0 + jnp.exp(-value))


def gate_up_kernel(ids_ref, *refs, steps, first, fetch):
    xs, refs = refs[: len(steps)], refs[len(steps) :]
    gate_weight, up_weight, *refs = refs
    down_weight, refs = (refs[0], refs[1:]) if fetch is not None else (None, refs)
    gate_in, up_in = (None, None) if first else refs[:2]
    refs = refs if first else refs[2:]
    gate_out, up_out, *refs = refs
    hold, sem = refs[-2 if fetch is None else -4 :][:2]
    width = xs[0].shape[1]
    blocks, tile = hold.shape[0], hold.shape[-1]

    def copy(n, which, step, into, signal):
        rows = pl.ds(pl.multiple_of(ids_ref[step] * width, width), width)
        columns = pl.ds(pl.multiple_of(n * tile, tile), tile)
        weight = (gate_weight, up_weight)[which]
        return pltpu.make_async_copy(weight.at[rows, columns], into, signal)

    def mine(n, which, j):
        into = hold.at[n, which, j * width : (j + 1) * width]
        return copy(n, which, steps[j], into, sem.at[n, which, j])

    def begin(n):
        for which in range(2):
            for j in range(len(steps)):
                mine(n, which, j).start()

    def block(n, carry):
        @pl.when(n + AHEAD < blocks)
        def _():
            begin(n + AHEAD)

        @pl.when(n == min(1, blocks - 1))
        def _():
            begin_ahead()

        at = pl.ds(pl.multiple_of(n * tile, tile), tile)
        x = jnp.concatenate([piece[...] for piece in xs], axis=1)
        for which in range(2):
            for j in range(len(steps)):
                mine(n, which, j).wait()
            value = dot(x, hold[n, which])
            if not first:
                value = (gate_in, up_in)[which][:, at] + value
            (gate_out, up_out)[which][:, at] = value
        return carry

    if fetch is not None:
        next_ref, down_ref, _, _, next_sem, down_sem = refs
        depth, breadth = down_ref.shape
        columns = pl.ds(pl.multiple_of(ids_ref[fetch] * breadth, breadth), breadth)
        below = pltpu.make_async_copy(down_weight.at[:, columns], down_ref, down_sem)

    def ahead(n, which):
        return copy(n, which, fetch, next_ref.at[n, which], next_sem.at[n, which])

    def begin_ahead():
        if fetch is not None:
            for n in range(blocks):
                for which in range(2):
                    ahead(n, which).start()
            below.start()

    for n in range(min(AHEAD, blocks)):
        begin(n)
    lax.fori_loop(0, blocks, block, 0)
    if fetch is not None:
        for n in range(blocks):
            for which in range(2):
                ahead(n, which).wait()
        below.wait()


def gate_up(ids, steps, xs, gate_weight, up_weight, sums, down_weight=None, fetch=None):
    slots, width = xs[0].shape
    hidden = gate_weight.shape[1]
    first = sums is None
    on_chip = pl.BlockSpec(memory_space=pltpu.VMEM)
    away = pl.BlockSpec(memory_space=pl.ANY)
    weights = [gate_weight, up_weight] + ([] if fetch is None else [down_weight])
    operands = [*xs, *weights, *([] if first else sums)]
    at = 1 + len(operands) - 2
    blocks = hidden // WIDE
    out_shape = [pltpu.VMEM((slots, hidden), F32)] * 2
    scratch = [
        pltpu.VMEM((blocks, 2, width * len(steps), WIDE), BF16),
        pltpu.SemaphoreType.DMA((blocks, 2, len(steps))),
    ]
    if fetch is not None:
        out_shape += [pltpu.VMEM((blocks, 2, width, WIDE), BF16), pltpu.VMEM((hidden, width), BF16)]
        scratch += [pltpu.SemaphoreType.DMA((blocks, 2)), pltpu.SemaphoreType.DMA]
    flops = 4 * slots * width * hidden * len(steps)
    moved = 4 * width * hidden * len(steps)
    return pl.pallas_call(
        functools.partial(gate_up_kernel, steps=steps, first=first, fetch=fetch),
        in_specs=[pl.BlockSpec(memory_space=pltpu.SMEM)]
        + [on_chip] * len(xs)
        + [away] * len(weights)
        + [on_chip] * (0 if first else 2),
        out_specs=[on_chip] * len(out_shape),
        out_shape=out_shape,
        scratch_shapes=scratch,
        input_output_aliases={} if first else {at: 0, at + 1: 1},
        compiler_params=params(),
        cost_estimate=pl.CostEstimate(flops=COST * flops, bytes_accessed=moved, transcendentals=0),
        name="gate_up",
    )(ids, *operands)


def turn_kernel(top_x, bottom_x, gate_in, up_in, next_ref, down_ref, hidden_ref, top_out, bottom_out):
    blocks, tile = next_ref.shape[0], next_ref.shape[-1]
    rows = top_out.shape[0]

    def block(n, carry):
        at = pl.ds(pl.multiple_of(n * tile, tile), tile)
        x = jnp.concatenate([top_x[...], bottom_x[...]], axis=0)
        gate = gate_in[:, at] + dot(x, next_ref[n, 0])
        up = up_in[:, at] + dot(x, next_ref[n, 1])
        hidden_ref[:, at] = (silu(gate) * up).astype(BF16)
        return carry

    def leave(n, carry):
        at = pl.ds(pl.multiple_of(n * TILE, TILE), TILE)
        value = dot(hidden_ref[...], down_ref[:, at])
        top_out[:, at] = value[:rows].astype(BF16)
        bottom_out[:, at] = value[rows:].astype(BF16)
        return carry

    lax.fori_loop(0, blocks, block, 0, unroll=True)
    lax.fori_loop(0, down_ref.shape[1] // TILE, leave, 0, unroll=True)


def turn(top, bottom, sums, next_weights, next_down):
    rows, width = top.shape
    hidden = sums[0].shape[1]
    on_chip = pl.BlockSpec(memory_space=pltpu.VMEM)
    return pl.pallas_call(
        turn_kernel,
        in_specs=[on_chip] * 6,
        out_specs=[on_chip] * 3,
        out_shape=[
            pltpu.VMEM((2 * rows, hidden), BF16),
            jax.ShapeDtypeStruct((rows, width), BF16),
            jax.ShapeDtypeStruct((rows, width), BF16),
        ],
        compiler_params=params(),
        cost_estimate=pl.CostEstimate(
            flops=12 * rows * width * hidden, bytes_accessed=0, transcendentals=0
        ),
        name="turn",
    )(top, bottom, *sums, next_weights, next_down)


def down_kernel(ids_ref, hidden_ref, weight_ref, *refs, steps):
    outs, hold, sem = refs[:-2], *refs[-2:]
    width = hold.shape[-1]
    depth = hidden_ref.shape[1]
    cuts = sem.shape[1]
    deep = depth // cuts

    def copy(i, k):
        columns = pl.ds(pl.multiple_of(ids_ref[steps[i]] * width, width), width)
        rows = slice(k * deep, (k + 1) * deep)
        return pltpu.make_async_copy(weight_ref.at[rows, columns], hold.at[i, rows], sem.at[i, k])

    for k in range(cuts):
        copy(0, k).start()
    for i in range(len(steps)):

        def block(n, carry, i=i):
            @pl.when(n == 0)
            def _():
                for k in range(cuts):
                    copy(i, k).wait()
                    if i + 1 < len(steps):
                        copy(i + 1, k).start()

            at = pl.ds(pl.multiple_of(n * TILE, TILE), TILE)
            outs[i][:, at] = dot(hidden_ref[...], hold[i, :, at])
            return carry

        lax.fori_loop(0, width // TILE, block, 0)


def down(ids, steps, hidden, down_weight, width):
    slots, depth = hidden.shape
    on_chip = pl.BlockSpec(memory_space=pltpu.VMEM)
    return pl.pallas_call(
        functools.partial(down_kernel, steps=steps),
        in_specs=[pl.BlockSpec(memory_space=pltpu.SMEM), on_chip, pl.BlockSpec(memory_space=pl.ANY)],
        out_specs=(on_chip,) * len(steps),
        out_shape=(jax.ShapeDtypeStruct((slots, width), F32),) * len(steps),
        scratch_shapes=[
            pltpu.VMEM((len(steps), depth, width), BF16),
            pltpu.SemaphoreType.DMA((len(steps), 4)),
        ],
        compiler_params=params(),
        cost_estimate=pl.CostEstimate(
            flops=COST * 2 * slots * depth * width * len(steps),
            bytes_accessed=2 * depth * width * len(steps),
            transcendentals=0,
        ),
        name="down",
    )(ids, hidden, down_weight)


def ring_of(size):
    return [*range(0, size, 2), *range(size - 1, 0, -2)]


def ring_plan(size, slots, tokens, expert_index, factor, gate_weight, up_weight, down_weight):
    width = tokens.shape[1]
    half = size // 2
    order = ring_of(size)
    table = [[order[(order.index(me) + s) % size] for s in range(size)] for me in range(size)]
    ids = jnp.asarray(table, jnp.int32)[lax.axis_index("tensor")]
    to_right = [(order[i], order[(i + 1) % size]) for i in range(size)]
    to_left = [(b, a) for a, b in to_right]

    def right_of(value):
        return lax.ppermute(value, "tensor", to_right)

    def left_of(value):
        return lax.ppermute(value, "tensor", to_left)

    def both(one, other):
        return lax.optimization_barrier((one, other))

    own, slot = compact(expert_index, tokens, slots)

    right, left = right_of(own), left_of(own)
    sums = gate_up(ids, [0], [own], gate_weight, up_weight, None)
    for s in range(1, half):
        here = [right, left]
        if s + 1 < half:
            right, left = right_of(right), left_of(left)
        else:
            right, left = right_of(right[: slots // 2]), left_of(left[slots // 2 :])
        if s == max(1, half - 2):
            *sums, next_weights, next_down = gate_up(
                ids, [size - s, s], here, gate_weight, up_weight, sums, down_weight, fetch=half
            )
        else:
            sums = gate_up(ids, [size - s, s], here, gate_weight, up_weight, sums)
    hidden, top, bottom = turn(right, left, sums, next_weights, next_down)

    right, left = both(right_of(top), left_of(bottom))
    for s in range(half - 1, 0, -1):
        ahead, behind = down(ids, [s, size - s], hidden, down_weight, width)
        if s == half - 1:
            rows = slots // 2
            ahead = jnp.concatenate([ahead[:rows] + right.astype(F32), ahead[rows:]])
            behind = jnp.concatenate([behind[:rows], behind[rows:] + left.astype(F32)])
        else:
            ahead = ahead + right.astype(F32)
            behind = behind + left.astype(F32)
        right, left = both(right_of(ahead.astype(BF16)), left_of(behind.astype(BF16)))
    (mine,) = down(ids, [0], hidden, down_weight, width)

    slot = slot.reshape(-1)
    slot_ids = jnp.arange(slots, dtype=jnp.int32)
    place = (slot[:, None] == slot_ids[None, :]).astype(BF16)
    scale = jnp.sum(jnp.where(slot_ids[:, None] == slot[None, :], factor[None, :], 0.0), axis=1)
    total = mine + right.astype(F32) + left.astype(F32)
    return dot(place, (total * scale[:, None]).astype(BF16)).astype(BF16)


def plain_plan(slots, tokens, routed, factor, gate_weight, up_weight, down_weight):
    slot = jnp.where(routed, jnp.cumsum(routed.astype(jnp.int32)) - 1, -1)
    slot_ids = jnp.arange(slots, dtype=jnp.int32)
    select = slot_ids[:, None] == slot[None, :]
    chosen = dot(select.astype(BF16), tokens).astype(BF16)
    scale = jnp.sum(jnp.where(select, factor[None, :], 0.0), axis=1)
    full = lax.all_gather(chosen, "tensor", axis=1, tiled=True)
    gate, up = dot(full, gate_weight), dot(full, up_weight)
    hidden = (jax.nn.silu(gate) * up).astype(BF16)
    partial = dot(hidden, down_weight) * scale[:, None]
    total = lax.psum_scatter(partial, "tensor", scatter_dimension=1, tiled=True)
    return dot(select.T.astype(BF16), total.astype(BF16)).astype(BF16)


def local(size, tokens, expert_index, combine_weight, gate_weight, up_weight, down_weight):
    chosen = expert_index == 0
    routed = jnp.any(chosen, axis=1)
    factor = jnp.sum(jnp.where(chosen, combine_weight, 0.0), axis=1)
    weights = (gate_weight, up_weight, down_weight)
    fits = (
        size >= 4
        and size % 2 == 0
        and tokens.shape[1] % TILE == 0
        and gate_weight.shape[1] % WIDE == 0
        and tokens.shape[0] % LANES == 0
    )
    if not fits:
        return plain_plan(MOST, tokens, routed, factor, *weights)
    return ring_plan(size, MOST, tokens, expert_index, factor, *weights)


def solution(mesh):
    rows = P(("parts", "dp"), "tensor")
    in_specs = (
        rows,
        P(("parts", "dp"), None),
        P(("parts", "dp"), None),
        P(None, "tensor"),
        P(None, "tensor"),
        P("tensor", None),
    )
    return jax.shard_map(
        functools.partial(local, mesh.shape["tensor"]),
        mesh=mesh,
        in_specs=in_specs,
        out_specs=rows,
        check_vma=False,
    )
```

```python
import functools

import jax
import jax.numpy as jnp
from jax import lax
from jax.experimental import pallas as pl
from jax.experimental.pallas import tpu as pltpu
from jax.sharding import PartitionSpec as P

MOST = 512
LANES = 128
TILE = 256
WIDE = 512
COST = 2
F32 = jnp.float32
BF16 = jnp.bfloat16
VMEM_BYTES = 28 * 1024 * 1024


def params():
    return pltpu.CompilerParams(vmem_limit_bytes=VMEM_BYTES)


def dot(a, b):
    return jnp.dot(a, b, preferred_element_type=F32)


def compact_kernel(named_ref, tokens_ref, chosen_ref, slot_ref, select_ref, held_ref, sem):
    slots, count = select_ref.shape
    groups = count // LANES
    cuts = sem.shape[0]
    deep = count // cuts

    def bring(k):
        rows = slice(k * deep, (k + 1) * deep)
        return pltpu.make_async_copy(tokens_ref.at[rows], held_ref.at[rows], sem.at[k])

    for k in range(cuts):
        bring(k).start()
    hits = jnp.max(jnp.where(named_ref[...] == 0, 1.0, 0.0), axis=0, keepdims=True)
    routed = jnp.concatenate([hits[:, g * LANES : (g + 1) * LANES] for g in range(groups)], axis=0)
    above = lax.broadcasted_iota(jnp.int32, (LANES, LANES), 0) <= lax.broadcasted_iota(
        jnp.int32, (LANES, LANES), 1
    )
    within = dot(routed.astype(BF16), jnp.where(above, 1.0, 0.0).astype(BF16))
    before = jnp.zeros((1, 1), F32)
    slot_ids = lax.broadcasted_iota(jnp.int32, (slots, LANES), 0)
    for g in range(groups):
        row = within[g : g + 1, :] + before
        before = row[:, LANES - 1 :]
        slot = jnp.where(routed[g : g + 1, :] > 0, row.astype(jnp.int32) - 1, -1)
        slot_ref[g : g + 1, :] = slot
        select_ref[:, g * LANES : (g + 1) * LANES] = jnp.where(slot_ids == slot, 1.0, 0.0).astype(BF16)
    for k in range(cuts):
        bring(k).wait()

    def pick(n, carry):
        at = pl.ds(pl.multiple_of(n * TILE, TILE), TILE)
        chosen_ref[:, at] = dot(select_ref[...], held_ref[:, at]).astype(BF16)
        return carry

    lax.fori_loop(0, held_ref.shape[1] // TILE, pick, 0)


def compact(expert_index, tokens, slots):
    count, width = tokens.shape
    groups = count // LANES
    return pl.pallas_call(
        compact_kernel,
        out_shape=(
            jax.ShapeDtypeStruct((slots, width), BF16),
            jax.ShapeDtypeStruct((groups, LANES), jnp.int32),
        ),
        in_specs=[pl.BlockSpec(memory_space=pltpu.VMEM), pl.BlockSpec(memory_space=pl.ANY)],
        scratch_shapes=[
            pltpu.VMEM((slots, count), BF16),
            pltpu.VMEM((count, width), BF16),
            pltpu.SemaphoreType.DMA((2,)),
        ],
        compiler_params=params(),
        name="compact",
    )(expert_index.T, pltpu.with_memory_space_constraint(tokens, pltpu.HBM))


def silu(value):
    return value / (1.0 + jnp.exp(-value))


def gate_up_kernel(ids_ref, *refs, steps, first, fetch, follow, given):
    xs, refs = refs[: len(steps)], refs[len(steps) :]
    gate_weight, up_weight, *refs = refs
    down_weight, refs = (refs[0], refs[1:]) if fetch is not None else (None, refs)
    gate_in, up_in = (None, None) if first else refs[:2]
    refs = refs if first else refs[2:]
    given_ref, refs = (refs[0], refs[1:]) if given else (None, refs)
    gate_out, up_out, *refs = refs
    if fetch is not None:
        next_ref, down_ref, *refs = refs
    if follow is not None:
        follow_ref, *refs = refs
    hold, sem, *sems = refs
    width = xs[0].shape[1]
    blocks, tile = hold.shape[0], hold.shape[-1]

    def copy(n, which, step, into, signal):
        rows = pl.ds(pl.multiple_of(ids_ref[step] * width, width), width)
        columns = pl.ds(pl.multiple_of(n * tile, tile), tile)
        weight = (gate_weight, up_weight)[which]
        return pltpu.make_async_copy(weight.at[rows, columns], into, signal)

    def mine(n, which, j):
        into = hold.at[n, which, j * width : (j + 1) * width]
        return copy(n, which, steps[j], into, sem.at[n, which, j])

    def begin(n):
        for which in range(2):
            for j in range(len(steps)):
                mine(n, which, j).start()

    def block(n, carry, ready=None):
        @pl.when(n == min(1, blocks - 1))
        def _():
            begin_ahead()

        at = pl.ds(pl.multiple_of(n * tile, tile), tile)
        x = jnp.concatenate([piece[...] for piece in xs], axis=1)
        for which in range(2):
            if ready is None:
                for j in range(len(steps)):
                    mine(n, which, j).wait()
            value = dot(x, hold[n, which] if ready is None else ready[which])
            if not first:
                value = (gate_in, up_in)[which][:, at] + value
            (gate_out, up_out)[which][:, at] = value
        return carry

    if fetch is not None:
        next_sem, down_sem = sems[:2]
        depth, breadth = down_ref.shape
        columns = pl.ds(pl.multiple_of(ids_ref[fetch] * breadth, breadth), breadth)
        below = pltpu.make_async_copy(down_weight.at[:, columns], down_ref, down_sem)

    def ahead(n, which):
        return copy(n, which, fetch, next_ref.at[n, which], next_sem.at[n, which])

    def after(which, j):
        width_at = slice(j * width, (j + 1) * width)
        return copy(0, which, follow[j], follow_ref.at[which, width_at], sems[2].at[which, j])

    def begin_ahead():
        if follow is not None:
            for which in range(2):
                for j in range(len(follow)):
                    after(which, j).start()
        if fetch is not None:
            for n in range(blocks):
                for which in range(2):
                    ahead(n, which).start()
            below.start()

    for n in range(1 if given else 0, blocks):
        begin(n)
    if given:
        block(0, 0, given_ref)
    lax.fori_loop(1 if given else 0, blocks, block, 0)
    if follow is not None:
        for which in range(2):
            for j in range(len(follow)):
                after(which, j).wait()
    if fetch is not None:
        for n in range(blocks):
            for which in range(2):
                ahead(n, which).wait()
        below.wait()


def gate_up(ids, steps, xs, gate_weight, up_weight, sums, down_weight=None, fetch=None, follow=None, given=None):
    slots, width = xs[0].shape
    hidden = gate_weight.shape[1]
    first = sums is None
    on_chip = pl.BlockSpec(memory_space=pltpu.VMEM)
    away = pl.BlockSpec(memory_space=pl.ANY)
    weights = [gate_weight, up_weight] + ([] if fetch is None else [down_weight])
    operands = [*xs, *weights, *([] if first else sums)]
    at = 1 + len(operands) - 2
    operands += [] if given is None else [given]
    blocks = hidden // WIDE
    out_shape = [pltpu.VMEM((slots, hidden), F32)] * 2
    scratch = [
        pltpu.VMEM((blocks, 2, width * len(steps), WIDE), BF16),
        pltpu.SemaphoreType.DMA((blocks, 2, len(steps))),
    ]
    if fetch is not None:
        out_shape += [pltpu.VMEM((blocks, 2, width, WIDE), BF16), pltpu.VMEM((hidden, width), BF16)]
        scratch += [pltpu.SemaphoreType.DMA((blocks, 2)), pltpu.SemaphoreType.DMA]
    if follow is not None:
        out_shape += [pltpu.VMEM((2, width * len(follow), WIDE), BF16)]
        scratch += [pltpu.SemaphoreType.DMA((2, len(follow)))]
    flops = 4 * slots * width * hidden * len(steps)
    moved = 4 * width * hidden * len(steps)
    return pl.pallas_call(
        functools.partial(
            gate_up_kernel, steps=steps, first=first, fetch=fetch, follow=follow, given=given is not None
        ),
        in_specs=[pl.BlockSpec(memory_space=pltpu.SMEM)]
        + [on_chip] * len(xs)
        + [away] * len(weights)
        + [on_chip] * (0 if first else 2)
        + [on_chip] * (0 if given is None else 1),
        out_specs=[on_chip] * len(out_shape),
        out_shape=out_shape,
        scratch_shapes=scratch,
        input_output_aliases={} if first else {at: 0, at + 1: 1},
        compiler_params=params(),
        cost_estimate=pl.CostEstimate(flops=COST * flops, bytes_accessed=moved, transcendentals=0),
        name="gate_up",
    )(ids, *operands)


def turn_kernel(top_x, bottom_x, gate_in, up_in, next_ref, down_ref, hidden_ref, top_out, bottom_out):
    blocks, tile = next_ref.shape[0], next_ref.shape[-1]
    rows = top_out.shape[0]

    def block(n, carry):
        at = pl.ds(pl.multiple_of(n * tile, tile), tile)
        x = jnp.concatenate([top_x[...], bottom_x[...]], axis=0)
        gate = gate_in[:, at] + dot(x, next_ref[n, 0])
        up = up_in[:, at] + dot(x, next_ref[n, 1])
        hidden_ref[:, at] = (silu(gate) * up).astype(BF16)
        return carry

    def leave(n, carry):
        at = pl.ds(pl.multiple_of(n * TILE, TILE), TILE)
        value = dot(hidden_ref[...], down_ref[:, at])
        top_out[:, at] = value[:rows].astype(BF16)
        bottom_out[:, at] = value[rows:].astype(BF16)
        return carry

    lax.fori_loop(0, blocks, block, 0, unroll=True)
    lax.fori_loop(0, down_ref.shape[1] // TILE, leave, 0, unroll=True)


def turn(top, bottom, sums, next_weights, next_down):
    rows, width = top.shape
    hidden = sums[0].shape[1]
    on_chip = pl.BlockSpec(memory_space=pltpu.VMEM)
    return pl.pallas_call(
        turn_kernel,
        in_specs=[on_chip] * 6,
        out_specs=[on_chip] * 3,
        out_shape=[
            pltpu.VMEM((2 * rows, hidden), BF16),
            jax.ShapeDtypeStruct((rows, width), BF16),
            jax.ShapeDtypeStruct((rows, width), BF16),
        ],
        compiler_params=params(),
        cost_estimate=pl.CostEstimate(
            flops=12 * rows * width * hidden, bytes_accessed=0, transcendentals=0
        ),
        name="turn",
    )(top, bottom, *sums, next_weights, next_down)


def down_kernel(ids_ref, hidden_ref, weight_ref, *refs, steps):
    outs, hold, sem = refs[:-2], *refs[-2:]
    width = hold.shape[-1]
    depth = hidden_ref.shape[1]
    cuts = sem.shape[1]
    deep = depth // cuts

    def copy(i, k):
        columns = pl.ds(pl.multiple_of(ids_ref[steps[i]] * width, width), width)
        rows = slice(k * deep, (k + 1) * deep)
        return pltpu.make_async_copy(weight_ref.at[rows, columns], hold.at[i, rows], sem.at[i, k])

    for k in range(cuts):
        copy(0, k).start()
    for i in range(len(steps)):

        def block(n, carry, i=i):
            @pl.when(n == 0)
            def _():
                for k in range(cuts):
                    copy(i, k).wait()
                    if i + 1 < len(steps):
                        copy(i + 1, k).start()

            at = pl.ds(pl.multiple_of(n * TILE, TILE), TILE)
            outs[i][:, at] = dot(hidden_ref[...], hold[i, :, at])
            return carry

        lax.fori_loop(0, width // TILE, block, 0)


def down(ids, steps, hidden, down_weight, width):
    slots, depth = hidden.shape
    on_chip = pl.BlockSpec(memory_space=pltpu.VMEM)
    return pl.pallas_call(
        functools.partial(down_kernel, steps=steps),
        in_specs=[pl.BlockSpec(memory_space=pltpu.SMEM), on_chip, pl.BlockSpec(memory_space=pl.ANY)],
        out_specs=(on_chip,) * len(steps),
        out_shape=(jax.ShapeDtypeStruct((slots, width), F32),) * len(steps),
        scratch_shapes=[
            pltpu.VMEM((len(steps), depth, width), BF16),
            pltpu.SemaphoreType.DMA((len(steps), 4)),
        ],
        compiler_params=params(),
        cost_estimate=pl.CostEstimate(
            flops=COST * 2 * slots * depth * width * len(steps),
            bytes_accessed=2 * depth * width * len(steps),
            transcendentals=0,
        ),
        name="down",
    )(ids, hidden, down_weight)


def ring_of(size):
    return [*range(0, size, 2), *range(size - 1, 0, -2)]


def ring_plan(size, slots, tokens, expert_index, factor, gate_weight, up_weight, down_weight):
    width = tokens.shape[1]
    half = size // 2
    order = ring_of(size)
    table = [[order[(order.index(me) + s) % size] for s in range(size)] for me in range(size)]
    ids = jnp.asarray(table, jnp.int32)[lax.axis_index("tensor")]
    to_right = [(order[i], order[(i + 1) % size]) for i in range(size)]
    to_left = [(b, a) for a, b in to_right]

    def right_of(value):
        return lax.ppermute(value, "tensor", to_right)

    def left_of(value):
        return lax.ppermute(value, "tensor", to_left)

    def both(one, other):
        return lax.optimization_barrier((one, other))

    own, slot = compact(expert_index, tokens, slots)

    right, left = right_of(own), left_of(own)
    sums, given = gate_up(ids, [0], [own], gate_weight, up_weight, None), None
    for s in range(1, half):
        here = [right, left]
        if s + 1 < half:
            right, left = right_of(right), left_of(left)
        else:
            right, left = right_of(right[: slots // 2]), left_of(left[slots // 2 :])
        if s == max(1, half - 2):
            follow = [size - s - 1, s + 1] if s + 1 < half else None
            gate, up, next_weights, next_down, *more = gate_up(
                ids, [size - s, s], here, gate_weight, up_weight, sums, down_weight, half, follow
            )
            sums, given = [gate, up], more[0] if more else None
        else:
            sums = gate_up(ids, [size - s, s], here, gate_weight, up_weight, sums, given=given)
    hidden, top, bottom = turn(right, left, sums, next_weights, next_down)

    right, left = both(right_of(top), left_of(bottom))
    for s in range(half - 1, 0, -1):
        ahead, behind = down(ids, [s, size - s], hidden, down_weight, width)
        if s == half - 1:
            rows = slots // 2
            ahead = jnp.concatenate([ahead[:rows] + right.astype(F32), ahead[rows:]])
            behind = jnp.concatenate([behind[:rows], behind[rows:] + left.astype(F32)])
        else:
            ahead = ahead + right.astype(F32)
            behind = behind + left.astype(F32)
        right, left = both(right_of(ahead.astype(BF16)), left_of(behind.astype(BF16)))
    (mine,) = down(ids, [0], hidden, down_weight, width)

    slot = slot.reshape(-1)
    slot_ids = jnp.arange(slots, dtype=jnp.int32)
    place = (slot[:, None] == slot_ids[None, :]).astype(BF16)
    scale = jnp.sum(jnp.where(slot_ids[:, None] == slot[None, :], factor[None, :], 0.0), axis=1)
    total = mine + right.astype(F32) + left.astype(F32)
    return dot(place, (total * scale[:, None]).astype(BF16)).astype(BF16)


def plain_plan(slots, tokens, routed, factor, gate_weight, up_weight, down_weight):
    slot = jnp.where(routed, jnp.cumsum(routed.astype(jnp.int32)) - 1, -1)
    slot_ids = jnp.arange(slots, dtype=jnp.int32)
    select = slot_ids[:, None] == slot[None, :]
    chosen = dot(select.astype(BF16), tokens).astype(BF16)
    scale = jnp.sum(jnp.where(select, factor[None, :], 0.0), axis=1)
    full = lax.all_gather(chosen, "tensor", axis=1, tiled=True)
    gate, up = dot(full, gate_weight), dot(full, up_weight)
    hidden = (jax.nn.silu(gate) * up).astype(BF16)
    partial = dot(hidden, down_weight) * scale[:, None]
    total = lax.psum_scatter(partial, "tensor", scatter_dimension=1, tiled=True)
    return dot(select.T.astype(BF16), total.astype(BF16)).astype(BF16)


def local(size, tokens, expert_index, combine_weight, gate_weight, up_weight, down_weight):
    chosen = expert_index == 0
    routed = jnp.any(chosen, axis=1)
    factor = jnp.sum(jnp.where(chosen, combine_weight, 0.0), axis=1)
    weights = (gate_weight, up_weight, down_weight)
    fits = (
        size >= 4
        and size % 2 == 0
        and tokens.shape[1] % TILE == 0
        and gate_weight.shape[1] % WIDE == 0
        and tokens.shape[0] % LANES == 0
    )
    if not fits:
        return plain_plan(MOST, tokens, routed, factor, *weights)
    return ring_plan(size, MOST, tokens, expert_index, factor, *weights)


def solution(mesh):
    rows = P(("parts", "dp"), "tensor")
    in_specs = (
        rows,
        P(("parts", "dp"), None),
        P(("parts", "dp"), None),
        P(None, "tensor"),
        P(None, "tensor"),
        P("tensor", None),
    )
    return jax.shard_map(
        functools.partial(local, mesh.shape["tensor"]),
        mesh=mesh,
        in_specs=in_specs,
        out_specs=rows,
        check_vma=False,
    )
```

```python
import functools

import jax
import jax.numpy as jnp
from jax import lax
from jax.experimental import pallas as pl
from jax.experimental.pallas import tpu as pltpu
from jax.sharding import PartitionSpec as P

MOST = 512
LANES = 128
TILE = 256
WIDE = 512
COST = 2
F32 = jnp.float32
BF16 = jnp.bfloat16
VMEM_BYTES = 28 * 1024 * 1024


def params():
    return pltpu.CompilerParams(vmem_limit_bytes=VMEM_BYTES)


def dot(a, b):
    return jnp.dot(a, b, preferred_element_type=F32)


def compact_kernel(named_ref, tokens_ref, chosen_ref, slot_ref, select_ref, held_ref, sem):
    slots, count = select_ref.shape
    groups = count // LANES
    cuts = sem.shape[0]
    deep = count // cuts

    def bring(k):
        rows = slice(k * deep, (k + 1) * deep)
        return pltpu.make_async_copy(tokens_ref.at[rows], held_ref.at[rows], sem.at[k])

    for k in range(cuts):
        bring(k).start()
    hits = jnp.max(jnp.where(named_ref[...] == 0, 1.0, 0.0), axis=0, keepdims=True)
    routed = jnp.concatenate([hits[:, g * LANES : (g + 1) * LANES] for g in range(groups)], axis=0)
    above = lax.broadcasted_iota(jnp.int32, (LANES, LANES), 0) <= lax.broadcasted_iota(
        jnp.int32, (LANES, LANES), 1
    )
    within = dot(routed.astype(BF16), jnp.where(above, 1.0, 0.0).astype(BF16))
    before = jnp.zeros((1, 1), F32)
    slot_ids = lax.broadcasted_iota(jnp.int32, (slots, LANES), 0)
    for g in range(groups):
        row = within[g : g + 1, :] + before
        before = row[:, LANES - 1 :]
        slot = jnp.where(routed[g : g + 1, :] > 0, row.astype(jnp.int32) - 1, -1)
        slot_ref[g : g + 1, :] = slot
        select_ref[:, g * LANES : (g + 1) * LANES] = jnp.where(slot_ids == slot, 1.0, 0.0).astype(BF16)
    for k in range(cuts):
        bring(k).wait()

    def pick(n, carry):
        at = pl.ds(pl.multiple_of(n * TILE, TILE), TILE)
        chosen_ref[:, at] = dot(select_ref[...], held_ref[:, at]).astype(BF16)
        return carry

    lax.fori_loop(0, held_ref.shape[1] // TILE, pick, 0)


def compact(expert_index, tokens, slots):
    count, width = tokens.shape
    groups = count // LANES
    return pl.pallas_call(
        compact_kernel,
        out_shape=(
            jax.ShapeDtypeStruct((slots, width), BF16),
            jax.ShapeDtypeStruct((groups, LANES), jnp.int32),
        ),
        in_specs=[pl.BlockSpec(memory_space=pltpu.VMEM), pl.BlockSpec(memory_space=pl.ANY)],
        scratch_shapes=[
            pltpu.VMEM((slots, count), BF16),
            pltpu.VMEM((count, width), BF16),
            pltpu.SemaphoreType.DMA((2,)),
        ],
        compiler_params=params(),
        name="compact",
    )(expert_index.T, pltpu.with_memory_space_constraint(tokens, pltpu.HBM))


def silu(value):
    return value / (1.0 + jnp.exp(-value))


def gate_up_kernel(ids_ref, *refs, steps, first, fetch, follow, given):
    xs, refs = refs[: len(steps)], refs[len(steps) :]
    gate_weight, up_weight, *refs = refs
    down_weight, refs = (refs[0], refs[1:]) if fetch is not None else (None, refs)
    gate_in, up_in = (None, None) if first else refs[:2]
    refs = refs if first else refs[2:]
    given_ref, refs = (refs[0], refs[1:]) if given else (None, refs)
    gate_out, up_out, *refs = refs
    if fetch is not None:
        next_ref, down_ref, *refs = refs
    if follow is not None:
        follow_ref, *refs = refs
    hold, sem, *sems = refs
    width = xs[0].shape[1]
    blocks, tile = hold.shape[0], hold.shape[-1]

    def copy(n, which, step, into, signal):
        rows = pl.ds(pl.multiple_of(ids_ref[step] * width, width), width)
        columns = pl.ds(pl.multiple_of(n * tile, tile), tile)
        weight = (gate_weight, up_weight)[which]
        return pltpu.make_async_copy(weight.at[rows, columns], into, signal)

    def mine(n, which, j):
        into = hold.at[n, which, j * width : (j + 1) * width]
        return copy(n, which, steps[j], into, sem.at[n, which, j])

    def begin(n):
        for which in range(2):
            for j in range(len(steps)):
                mine(n, which, j).start()

    def block(n, carry, ready=None):
        @pl.when(n == min(1, blocks - 1))
        def _():
            begin_ahead()

        at = pl.ds(pl.multiple_of(n * tile, tile), tile)
        x = jnp.concatenate([piece[...] for piece in xs], axis=1)
        for which in range(2):
            if ready is None:
                for j in range(len(steps)):
                    mine(n, which, j).wait()
            value = dot(x, hold[n, which] if ready is None else ready[which])
            if not first:
                value = (gate_in, up_in)[which][:, at] + value
            (gate_out, up_out)[which][:, at] = value
        return carry

    if fetch is not None:
        next_sem, down_sem = sems[:2]
        depth, breadth = down_ref.shape
        columns = pl.ds(pl.multiple_of(ids_ref[fetch] * breadth, breadth), breadth)
        below = pltpu.make_async_copy(down_weight.at[:, columns], down_ref, down_sem)

    def ahead(n, which):
        return copy(n, which, fetch, next_ref.at[n, which], next_sem.at[n, which])

    def after(which, j):
        width_at = slice(j * width, (j + 1) * width)
        return copy(0, which, follow[j], follow_ref.at[which, width_at], sems[2].at[which, j])

    def begin_ahead():
        if follow is not None:
            for which in range(2):
                for j in range(len(follow)):
                    after(which, j).start()
        if fetch is not None:
            for n in range(blocks):
                for which in range(2):
                    ahead(n, which).start()
            below.start()

    for n in range(1 if given else 0, blocks):
        begin(n)
    if given:
        block(0, 0, given_ref)
    lax.fori_loop(1 if given else 0, blocks, block, 0)
    if follow is not None:
        for which in range(2):
            for j in range(len(follow)):
                after(which, j).wait()
    if fetch is not None:
        for n in range(blocks):
            for which in range(2):
                ahead(n, which).wait()
        below.wait()


def gate_up(ids, steps, xs, gate_weight, up_weight, sums, down_weight=None, fetch=None, follow=None, given=None):
    slots, width = xs[0].shape
    hidden = gate_weight.shape[1]
    first = sums is None
    on_chip = pl.BlockSpec(memory_space=pltpu.VMEM)
    away = pl.BlockSpec(memory_space=pl.ANY)
    weights = [gate_weight, up_weight] + ([] if fetch is None else [down_weight])
    operands = [*xs, *weights, *([] if first else sums)]
    at = 1 + len(operands) - 2
    operands += [] if given is None else [given]
    blocks = hidden // WIDE
    out_shape = [pltpu.VMEM((slots, hidden), F32)] * 2
    scratch = [
        pltpu.VMEM((blocks, 2, width * len(steps), WIDE), BF16),
        pltpu.SemaphoreType.DMA((blocks, 2, len(steps))),
    ]
    if fetch is not None:
        out_shape += [pltpu.VMEM((blocks, 2, width, WIDE), BF16), pltpu.VMEM((hidden, width), BF16)]
        scratch += [pltpu.SemaphoreType.DMA((blocks, 2)), pltpu.SemaphoreType.DMA]
    if follow is not None:
        out_shape += [pltpu.VMEM((2, width * len(follow), WIDE), BF16)]
        scratch += [pltpu.SemaphoreType.DMA((2, len(follow)))]
    flops = 4 * slots * width * hidden * len(steps)
    moved = 4 * width * hidden * len(steps)
    return pl.pallas_call(
        functools.partial(
            gate_up_kernel, steps=steps, first=first, fetch=fetch, follow=follow, given=given is not None
        ),
        in_specs=[pl.BlockSpec(memory_space=pltpu.SMEM)]
        + [on_chip] * len(xs)
        + [away] * len(weights)
        + [on_chip] * (0 if first else 2)
        + [on_chip] * (0 if given is None else 1),
        out_specs=[on_chip] * len(out_shape),
        out_shape=out_shape,
        scratch_shapes=scratch,
        input_output_aliases={} if first else {at: 0, at + 1: 1},
        compiler_params=params(),
        cost_estimate=pl.CostEstimate(flops=COST * flops, bytes_accessed=moved, transcendentals=0),
        name="gate_up",
    )(ids, *operands)


def turn_kernel(top_x, bottom_x, gate_in, up_in, next_ref, down_ref, hidden_ref, top_out, bottom_out):
    blocks, tile = next_ref.shape[0], next_ref.shape[-1]
    rows = top_out.shape[0]

    def block(n, carry):
        at = pl.ds(pl.multiple_of(n * tile, tile), tile)
        x = jnp.concatenate([top_x[...], bottom_x[...]], axis=0)
        gate = gate_in[:, at] + dot(x, next_ref[n, 0])
        up = up_in[:, at] + dot(x, next_ref[n, 1])
        hidden_ref[:, at] = (silu(gate) * up).astype(BF16)
        return carry

    def leave(n, carry):
        at = pl.ds(pl.multiple_of(n * TILE, TILE), TILE)
        value = dot(hidden_ref[...], down_ref[:, at])
        top_out[:, at] = value[:rows].astype(BF16)
        bottom_out[:, at] = value[rows:].astype(BF16)
        return carry

    lax.fori_loop(0, blocks, block, 0, unroll=True)
    lax.fori_loop(0, down_ref.shape[1] // TILE, leave, 0, unroll=True)


def turn(top, bottom, sums, next_weights, next_down):
    rows, width = top.shape
    hidden = sums[0].shape[1]
    on_chip = pl.BlockSpec(memory_space=pltpu.VMEM)
    return pl.pallas_call(
        turn_kernel,
        in_specs=[on_chip] * 6,
        out_specs=[on_chip] * 3,
        out_shape=[
            pltpu.VMEM((2 * rows, hidden), BF16),
            jax.ShapeDtypeStruct((rows, width), BF16),
            jax.ShapeDtypeStruct((rows, width), BF16),
        ],
        compiler_params=params(),
        cost_estimate=pl.CostEstimate(
            flops=12 * rows * width * hidden, bytes_accessed=0, transcendentals=0
        ),
        name="turn",
    )(top, bottom, *sums, next_weights, next_down)


def down_kernel(ids_ref, hidden_ref, weight_ref, out_ref, hold, sem, *, steps):
    width = hold.shape[-1]
    depth = hidden_ref.shape[1]
    cuts = sem.shape[1]
    deep = depth // cuts
    tiles = width // TILE

    def copy(i, k, step):
        columns = pl.ds(pl.multiple_of(ids_ref[step] * width, width), width)
        rows = slice(k * deep, (k + 1) * deep)
        return pltpu.make_async_copy(weight_ref.at[rows, columns], hold.at[i, rows], sem.at[i, k])

    def block(t, carry):
        i, n = t // tiles, t % tiles

        @pl.when(n == 0)
        def _():
            for k in range(cuts):
                copy(i, k, steps[0]).wait()

        at = pl.ds(pl.multiple_of(n * TILE, TILE), TILE)
        out_ref[i, :, at] = dot(hidden_ref[...], hold[i, :, at])
        return carry

    for i, step in enumerate(steps):
        for k in range(cuts):
            copy(i, k, step).start()
    lax.fori_loop(0, len(steps) * tiles, block, 0)


def down(ids, steps, hidden, down_weight, width):
    slots, depth = hidden.shape
    on_chip = pl.BlockSpec(memory_space=pltpu.VMEM)
    return pl.pallas_call(
        functools.partial(down_kernel, steps=steps),
        in_specs=[pl.BlockSpec(memory_space=pltpu.SMEM), on_chip, pl.BlockSpec(memory_space=pl.ANY)],
        out_specs=on_chip,
        out_shape=jax.ShapeDtypeStruct((len(steps), slots, width), F32),
        scratch_shapes=[
            pltpu.VMEM((len(steps), depth, width), BF16),
            pltpu.SemaphoreType.DMA((len(steps), 4)),
        ],
        compiler_params=params(),
        cost_estimate=pl.CostEstimate(
            flops=COST * 2 * slots * depth * width * len(steps),
            bytes_accessed=2 * depth * width * len(steps),
            transcendentals=0,
        ),
        name="down",
    )(ids, hidden, down_weight)


def ring_of(size):
    return [*range(0, size, 2), *range(size - 1, 0, -2)]


def ring_plan(size, slots, tokens, expert_index, factor, gate_weight, up_weight, down_weight):
    width = tokens.shape[1]
    half = size // 2
    order = ring_of(size)
    table = [[order[(order.index(me) + s) % size] for s in range(size)] for me in range(size)]
    ids = jnp.asarray(table, jnp.int32)[lax.axis_index("tensor")]
    to_right = [(order[i], order[(i + 1) % size]) for i in range(size)]
    to_left = [(b, a) for a, b in to_right]

    def right_of(value):
        return lax.ppermute(value, "tensor", to_right)

    def left_of(value):
        return lax.ppermute(value, "tensor", to_left)

    def both(one, other):
        return lax.optimization_barrier((one, other))

    own, slot = compact(expert_index, tokens, slots)

    right, left = right_of(own), left_of(own)
    sums, given = gate_up(ids, [0], [own], gate_weight, up_weight, None), None
    for s in range(1, half):
        here = [right, left]
        if s + 1 < half:
            right, left = right_of(right), left_of(left)
        else:
            right, left = right_of(right[: slots // 2]), left_of(left[slots // 2 :])
        if s == max(1, half - 2):
            follow = [size - s - 1, s + 1] if s + 1 < half else None
            gate, up, next_weights, next_down, *more = gate_up(
                ids, [size - s, s], here, gate_weight, up_weight, sums, down_weight, half, follow
            )
            sums, given = [gate, up], more[0] if more else None
        else:
            sums = gate_up(ids, [size - s, s], here, gate_weight, up_weight, sums, given=given)
    hidden, top, bottom = turn(right, left, sums, next_weights, next_down)

    right, left = both(right_of(top), left_of(bottom))
    for s in range(half - 1, 0, -1):
        ahead, behind = down(ids, [s, size - s], hidden, down_weight, width)
        if s == half - 1:
            rows = slots // 2
            ahead = jnp.concatenate([ahead[:rows] + right.astype(F32), ahead[rows:]])
            behind = jnp.concatenate([behind[:rows], behind[rows:] + left.astype(F32)])
        else:
            ahead = ahead + right.astype(F32)
            behind = behind + left.astype(F32)
        right, left = both(right_of(ahead.astype(BF16)), left_of(behind.astype(BF16)))
    (mine,) = down(ids, [0], hidden, down_weight, width)

    slot = slot.reshape(-1)
    slot_ids = jnp.arange(slots, dtype=jnp.int32)
    place = (slot[:, None] == slot_ids[None, :]).astype(BF16)
    scale = jnp.sum(jnp.where(slot_ids[:, None] == slot[None, :], factor[None, :], 0.0), axis=1)
    total = mine + right.astype(F32) + left.astype(F32)
    return dot(place, (total * scale[:, None]).astype(BF16)).astype(BF16)


def plain_plan(slots, tokens, routed, factor, gate_weight, up_weight, down_weight):
    slot = jnp.where(routed, jnp.cumsum(routed.astype(jnp.int32)) - 1, -1)
    slot_ids = jnp.arange(slots, dtype=jnp.int32)
    select = slot_ids[:, None] == slot[None, :]
    chosen = dot(select.astype(BF16), tokens).astype(BF16)
    scale = jnp.sum(jnp.where(select, factor[None, :], 0.0), axis=1)
    full = lax.all_gather(chosen, "tensor", axis=1, tiled=True)
    gate, up = dot(full, gate_weight), dot(full, up_weight)
    hidden = (jax.nn.silu(gate) * up).astype(BF16)
    partial = dot(hidden, down_weight) * scale[:, None]
    total = lax.psum_scatter(partial, "tensor", scatter_dimension=1, tiled=True)
    return dot(select.T.astype(BF16), total.astype(BF16)).astype(BF16)


def local(size, tokens, expert_index, combine_weight, gate_weight, up_weight, down_weight):
    chosen = expert_index == 0
    routed = jnp.any(chosen, axis=1)
    factor = jnp.sum(jnp.where(chosen, combine_weight, 0.0), axis=1)
    weights = (gate_weight, up_weight, down_weight)
    fits = (
        size >= 4
        and size % 2 == 0
        and tokens.shape[1] % TILE == 0
        and gate_weight.shape[1] % WIDE == 0
        and tokens.shape[0] % LANES == 0
    )
    if not fits:
        return plain_plan(MOST, tokens, routed, factor, *weights)
    return ring_plan(size, MOST, tokens, expert_index, factor, *weights)


def solution(mesh):
    rows = P(("parts", "dp"), "tensor")
    in_specs = (
        rows,
        P(("parts", "dp"), None),
        P(("parts", "dp"), None),
        P(None, "tensor"),
        P(None, "tensor"),
        P("tensor", None),
    )
    return jax.shard_map(
        functools.partial(local, mesh.shape["tensor"]),
        mesh=mesh,
        in_specs=in_specs,
        out_specs=rows,
        check_vma=False,
    )
```
